32 devices in a mesh: users: 8 (over z, x), rb: 4 (over y, core).
Axes of the slice: x: 2, y: 2, z: 4, core: 2. Of those that a mesh axis runs over, the one named last changes fastest.
Arguments:
- channel: bfloat16 [8192, 16, 3, 128], P('users', 'rb'), may hold values from -13 to 13
- serving: int32 [8192], P('users'), may hold values from 0 to 15, as said below
- interferers: int32 [8192, 2], P('users'), may hold values from 0 to 15, as said below
- plan: int32 [16, 16, 16], P(None, 'rb'), may hold values from 0 to 8191, as said below
- regularizer: float32 [16], P('users'), may hold values from 0.3 to 1.5
- noise_floor: float32 [16], replicated, may hold values from 0.05 to 0.5
Outputs:
- precoders: bfloat16 [16, 16, 16, 128], P('users', 'rb')
- track_metric: float32 [8192, 16], P('users', 'rb')
- entry_rate: float32 [16, 16, 16], P('users', 'rb')
The draws below stay inside these ranges and needn't reach their ends.
Inputs may be any that keep to these rules, and one draw needn't show every extreme that they name: `serving`: each aligned block of 1024 tracks holds exactly 64 tracks served by each cell. `interferers`: A track's 2 interfering cells differ from each other and from its serving cell; each aligned block of 1024 tracks holds exactly 64 tracks with a given cell in a given column. `plan`: each entry names a track served by that cell, and the 16 tracks of a cell on one resource block differ. Take a cell group g (cells g * 2 to g * 2 + 1) and an aligned block of 4 resource blocks: at most 32 of its entries name tracks of one aligned block of 1024 tracks.
All inputs are finite; a program needn't handle non-finite values.
Results may differ from the reference program's by a relative error of at most 0.0035.
Values may be sent and summed in bfloat16 or wider, within the bound.
A program may use at most 64 MiB of HBM per device.

```python
import math
import jax
import jax.numpy as jnp
from jax import lax

ANTENNA_COUNT = 64
BEAMS = 16
NI = 2
HEARD_CELLS = 3
ITERS = 12
CELL_DEV = 2
CELL_TOTAL = 16
TRACK_DEV = 1024
USER_TRACKS = 8192
SERVED = 64
RB_DEV = 4
RESOURCE_BLOCKS = 16
CAP = 32


def track_layout(key):
    groups = USER_TRACKS // TRACK_DEV
    perm_keys = jax.random.split(jax.random.fold_in(key, 11), groups)
    placement = jax.vmap(lambda one_key: jax.random.permutation(one_key, TRACK_DEV))(perm_keys).astype(jnp.int32)
    home_cell = placement // SERVED
    within = placement % SERVED
    shift_keys = jax.random.split(jax.random.fold_in(key, 12), groups * SERVED)
    shifts = jax.vmap(lambda one_key: jax.random.permutation(one_key, CELL_TOTAL - 1))(shift_keys).astype(jnp.int32)
    shifts = (shifts[:, :NI] + 1).reshape(groups, SERVED, NI)
    group_index = jnp.arange(groups, dtype=jnp.int32)[:, None]
    track_shift = shifts[group_index, within]
    hearing = (home_cell[:, :, None] + track_shift) % CELL_TOTAL
    inverse = jnp.zeros_like(placement).at[group_index, placement].set(jnp.broadcast_to(jnp.arange(TRACK_DEV, dtype=jnp.int32)[None, :], placement.shape))
    return (home_cell.reshape(USER_TRACKS), hearing.reshape(USER_TRACKS, NI), inverse)


def draw_serving(key, part):
    return track_layout(key)[0].astype(jnp.int32)


def draw_interferers(key, part):
    return track_layout(key)[1].astype(jnp.int32)


def draw_plan(key, part):
    groups = USER_TRACKS // TRACK_DEV
    rb_groups = RESOURCE_BLOCKS // RB_DEV
    entries = CELL_DEV * RB_DEV * BEAMS
    half_cap = CAP // 2
    inverse = track_layout(key)[2]
    block_keys = jax.random.split(jax.random.fold_in(key, 21), groups * rb_groups)
    dest_groups = jnp.repeat(jnp.arange(groups, dtype=jnp.int32), rb_groups)
    entry_iota = jnp.arange(entries, dtype=jnp.int32)

    def one_block(block_key, dest_group):
        pair_key, tilt_key, order_key = jax.random.split(block_key, 3)
        pairing = jax.random.permutation(pair_key, groups).astype(jnp.int32)
        tilt_amount = jax.random.randint(tilt_key, (groups // 2,), 0, half_cap + 1).astype(jnp.int32)
        tilt_amount = tilt_amount.at[0].set(half_cap)
        counts = jnp.zeros((groups,), jnp.int32).at[pairing[0::2]].set(half_cap + tilt_amount)
        counts = counts.at[pairing[1::2]].set(half_cap - tilt_amount)
        count_ends = jnp.cumsum(counts)
        sorted_source = jnp.sum((count_ends[None, :] <= entry_iota[:, None]).astype(jnp.int32), axis=1)
        shuffled = sorted_source[jax.random.permutation(order_key, entries)]
        cell_local = entry_iota // (RB_DEV * BEAMS)
        bucket = shuffled * CELL_DEV + cell_local
        bucket_match = (bucket[:, None] == jnp.arange(groups * CELL_DEV, dtype=jnp.int32)[None, :]).astype(jnp.int32)
        slot_rank = jnp.sum((jnp.cumsum(bucket_match, axis=0) - 1) * bucket_match, axis=1)
        cell_global = dest_group * CELL_DEV + cell_local
        return shuffled * TRACK_DEV + inverse[shuffled, cell_global * SERVED + slot_rank]
    table = jax.vmap(one_block)(block_keys, dest_groups)
    table = table.reshape(groups, rb_groups, CELL_DEV, RB_DEV, BEAMS).transpose(0, 2, 1, 3, 4)
    return table.reshape(CELL_TOTAL, RESOURCE_BLOCKS, BEAMS).astype(jnp.int32)


def draw_channel(key, part):
    amp_key, element_key = jax.random.split(key, 2)
    ramp = jnp.arange(RESOURCE_BLOCKS, dtype=jnp.float32) / max(RESOURCE_BLOCKS - 1, 1)
    amplitude = jnp.exp(jax.random.uniform(amp_key, (USER_TRACKS, 1, HEARD_CELLS, 1), jnp.float32, jnp.log(0.3), jnp.log(3.0)))
    profile = 0.6 + 0.8 * ramp
    element_values = jnp.clip(jax.random.normal(element_key, (USER_TRACKS, RESOURCE_BLOCKS, HEARD_CELLS, 2 * ANTENNA_COUNT), jnp.float32), -4.0, 4.0) * 0.70710677
    return (amplitude * profile[None, :, None, None] * element_values).astype(jnp.bfloat16)


def block_levels(rng, extent, pieces, least, largest):
    loudness, own = 1.0, jax.random.fold_in(rng, 6)
    for dim, shards_of in pieces:
        steps = jnp.exp(jax.random.uniform(jax.random.fold_in(own, dim), (shards_of,), jnp.float32, least / len(pieces), largest / len(pieces)))
        loudness = loudness * jnp.repeat(steps, extent[dim] // shards_of).reshape([-1 if axis == dim else 1 for axis in range(len(extent))])
    return loudness


def setup_inputs(seed: int = 0) -> dict:
    key_list = jax.random.split(jax.random.key(seed), 7)
    return {
        "channel": draw_channel(jax.random.fold_in(key_list[6], 71), 0),
        "serving": draw_serving(jax.random.fold_in(key_list[6], 71), 0),
        "interferers": draw_interferers(jax.random.fold_in(key_list[6], 71), 0),
        "plan": draw_plan(jax.random.fold_in(key_list[6], 71), 0),
        "regularizer": jnp.clip(jnp.exp(math.log(1.5) - 1.60943787 * jax.random.uniform(key_list[4], (CELL_TOTAL,), jnp.float32) ** block_levels(key_list[4], (CELL_TOTAL,), ((0, 8),), -0.2, 0.2)), 0.3, 1.5),
        "noise_floor": jnp.clip(jnp.exp(jax.random.uniform(key_list[5], (CELL_TOTAL,), jnp.float32, math.log(0.05), math.log(0.5))), 0.05, 0.5),
    }


HIGH = lax.Precision.HIGHEST

def real_form(beam_rows):
    antennas = beam_rows.shape[-1] // 2
    turned = jnp.concatenate([beam_rows[..., antennas:], -beam_rows[..., :antennas]], axis=-1)
    return jnp.concatenate([beam_rows, turned], axis=-2)

def embed_rows(channel_rows):
    antennas = channel_rows.shape[-1] // 2
    bottom_rows = jnp.concatenate([-channel_rows[..., antennas:], channel_rows[..., :antennas]], axis=-1)
    return jnp.concatenate([channel_rows, bottom_rows], axis=-2)

def unscaled_beams(sched_rows, regularizer):
    beam_count = sched_rows.shape[-2]
    embedded = embed_rows(sched_rows.astype(jnp.float32))
    gram = jnp.einsum('crkd,crjd->crkj', embedded, embedded, precision=HIGH)
    identity = jnp.eye(2 * beam_count, dtype=jnp.float32)
    gram = gram + regularizer[:, None, None, None] * identity
    gram_trace = jnp.trace(gram, axis1=2, axis2=3)
    start_inverse = (2.0 / gram_trace)[:, :, None, None] * identity

    def newton_step(iteration, inverse):
        product = jnp.einsum('crkj,crjl->crkl', gram, inverse, precision=HIGH)
        return 2.0 * inverse - jnp.einsum('crkj,crjl->crkl', inverse, product, precision=HIGH)
    inverse = lax.fori_loop(0, ITERS, newton_step, start_inverse)
    return jnp.einsum('crkd,crkj->crjd', embedded, inverse[..., :beam_count], precision=HIGH)

def reference(channel, serving, interferers, plan, regularizer, noise_floor):
    block_index = jnp.arange(RESOURCE_BLOCKS, dtype=jnp.int32)[None, :, None]
    sched_rows = channel[plan, block_index, 0]
    vectors = unscaled_beams(sched_rows, regularizer)
    cell_power = lax.optimization_barrier(jnp.sum(vectors * vectors, axis=(1, 2, 3)))
    precoders = (vectors * lax.rsqrt(cell_power / RESOURCE_BLOCKS + 1e-06)[:, None, None, None]).astype(jnp.bfloat16)
    forms = real_form(precoders)
    track_iota = jnp.arange(USER_TRACKS, dtype=jnp.int32)
    slot_cells = jnp.concatenate([serving[:, None], interferers], axis=1).T
    orders = jnp.argsort(slot_cells * USER_TRACKS + track_iota[None, :], axis=1).astype(jnp.int32)
    ranks = jnp.zeros_like(orders).at[jnp.arange(HEARD_CELLS, dtype=jnp.int32)[:, None], orders].set(jnp.broadcast_to(track_iota[None, :], orders.shape))
    cell_share = USER_TRACKS // CELL_TOTAL

    def block_powers(block_number):
        form_block = lax.dynamic_index_in_dim(forms, block_number, axis=1, keepdims=False).astype(jnp.float32)
        results = []
        for slot_number in range(HEARD_CELLS):
            track_row_list = channel[orders[slot_number], block_number, slot_number].astype(jnp.float32)
            track_row_list = track_row_list.reshape(CELL_TOTAL, cell_share, 2 * ANTENNA_COUNT)
            projected = jnp.einsum('cpd,ckd->cpk', track_row_list, form_block)
            grouped = lax.optimization_barrier(jnp.sum(projected * projected, axis=-1)).reshape(USER_TRACKS)
            results.append(grouped[ranks[slot_number]])
        return jnp.stack(results)
    powers = lax.map(block_powers, jnp.arange(RESOURCE_BLOCKS, dtype=jnp.int32))
    interference = powers[:, 1]
    for slot_number in range(2, HEARD_CELLS):
        interference = interference + powers[:, slot_number]
    denominator = interference + noise_floor[serving][None, :]
    track_metric = jnp.log2(1.0 + powers[:, 0] / denominator).T
    crossed = jnp.einsum('crkd,crjd->crkj', sched_rows.astype(jnp.float32), forms.astype(jnp.float32))
    magnitude = crossed[..., :BEAMS] * crossed[..., :BEAMS] + crossed[..., BEAMS:] * crossed[..., BEAMS:]
    identity = jnp.eye(BEAMS, dtype=jnp.float32)
    signal = lax.optimization_barrier(jnp.sum(magnitude * identity, axis=-1))
    leakage = lax.optimization_barrier(jnp.sum(magnitude * (1.0 - identity), axis=-1))
    entry_denominator = denominator.T[plan, block_index]
    entry_rate = jnp.log2(1.0 + signal / (leakage + entry_denominator))
    return (precoders, track_metric, entry_rate)
```

```python
import functools

import jax
import jax.numpy as jnp
from jax import lax
from jax.experimental import pallas as pl
from jax.experimental.pallas import tpu as pltpu
from jax.sharding import PartitionSpec as P

ITERS = 12
F32 = jnp.float32
BF16 = jnp.bfloat16
HIGH = lax.Precision.HIGHEST


def iota(shape, dim):
    return lax.broadcasted_iota(jnp.int32, shape, dim)


def log2_of(n):
    assert n & (n - 1) == 0
    return n.bit_length() - 1


def turn(rows):
    half = rows.shape[-1] // 2
    sign = jnp.where(iota(rows.shape, 1) < half, 1.0, -1.0)
    return pltpu.roll(rows, half, 1) * sign


def dot_nt(a, b):
    return lax.dot_general(a, b, (((1,), (1,)), ((), ())), preferred_element_type=F32)


def dot_nn(a, b):
    return jnp.dot(a, b, preferred_element_type=F32)


def split3(x):
    high = x.astype(BF16)
    rest = x - high.astype(F32)
    middle = rest.astype(BF16)
    return high, middle, (rest - middle.astype(F32)).astype(BF16)


def dot_split(x, b):
    high, middle, low = split3(x)
    return dot_nn(low, b) + dot_nn(middle, b) + dot_nn(high, b)


def spread(a, beams):
    lane = iota(a.shape, 1)
    base = lane - (lane & (beams - 1))
    return lambda m: jnp.take_along_axis(a, base + m, axis=1, mode="promise_in_bounds")


def complex_product(left_r, left_i, right_r, right_i, beams):
    out_r = out_i = None
    for m in range(beams):
        lr, li = left_r(m), left_i(m)
        rr, ri = right_r[m : m + 1, :], right_i[m : m + 1, :]
        term_r = lr * rr - li * ri
        term_i = lr * ri + li * rr
        out_r = term_r if out_r is None else out_r + term_r
        out_i = term_i if out_i is None else out_i + term_i
    return out_r, out_i


def newton_inverse(gram_r, gram_i, reg_lanes, beams):
    shape = gram_r.shape
    lanes = shape[1]
    shift = log2_of(beams)
    diagonal = (iota(shape, 1) & (beams - 1)) == iota(shape, 0)
    gram_r = gram_r + jnp.where(diagonal, reg_lanes, 0.0)
    diag_row = jnp.sum(jnp.where(diagonal, gram_r, 0.0), axis=0, keepdims=True)
    same = (iota((lanes, lanes), 0) >> shift) == (iota((lanes, lanes), 1) >> shift)
    trace = jnp.dot(
        jnp.broadcast_to(diag_row, (8, lanes)),
        jnp.where(same, 1.0, 0.0),
        precision=HIGH,
        preferred_element_type=F32,
    )[0:1, :]
    start_r = jnp.where(diagonal, 1.0 / trace, 0.0)
    start_i = jnp.zeros(shape, F32)
    gather_r, gather_i = spread(gram_r, beams), spread(gram_i, beams)
    held_r = [gather_r(m) for m in range(beams)]
    held_i = [gather_i(m) for m in range(beams)]

    def step(_, carry):
        xr, xi = carry
        yr, yi = complex_product(lambda m: held_r[m], lambda m: held_i[m], xr, xi, beams)
        zr, zi = complex_product(spread(xr, beams), spread(xi, beams), yr, yi, beams)
        return 2.0 * xr - zr, 2.0 * xi - zi

    return lax.fori_loop(0, ITERS, step, (start_r, start_i))


def kernel(
    dims,
    ch_ref,
    ent_ref,
    cells_ref,
    reg_ref,
    noise_ref,
    prec_ref,
    metric_ref,
    rate_ref,
    wide,
    planes,
    out_rows,
    in_rows,
    own_w,
    all_w,
    forms,
    received,
    pw_own,
    pw_in,
    dn_own,
    dn_in,
    row_send,
    row_recv,
    w_send,
    w_recv,
    pw_send,
    pw_recv,
    dn_send,
    dn_recv,
):
    groups, rb_groups, tracks, blocks, slots, cells, beams, cell_dev, capacity = dims
    entries = cell_dev * blocks * beams
    width = ch_ref.shape[1]
    track_shift = log2_of(tracks)
    beam_shift = log2_of(beams)
    me = lax.axis_index("users")
    my_rb = lax.axis_index("rb")

    barrier = pltpu.get_barrier_semaphore()
    for offset in range(1, groups):
        pl.semaphore_signal(
            barrier, inc=1, device_id={"users": lax.rem(me + offset, groups)},
            device_id_type=pl.DeviceIdType.MESH,
        )
    for offset in range(1, rb_groups):
        pl.semaphore_signal(
            barrier, inc=1, device_id={"rb": lax.rem(my_rb + offset, rb_groups)},
            device_id_type=pl.DeviceIdType.MESH,
        )

    def user_copy(src, dst, send, recv, offset):
        return pltpu.make_async_remote_copy(
            src_ref=src,
            dst_ref=dst,
            send_sem=send.at[offset],
            recv_sem=recv.at[offset],
            device_id={"users": lax.rem(me + offset, groups)},
            device_id_type=pl.DeviceIdType.MESH,
        )

    stride = slots * blocks
    rows = ch_ref.shape[0]
    chunk = rows // 8

    def widen(i, carry):
        part = pl.ds(pl.multiple_of(i * chunk, chunk), chunk)
        wide[part, :] = ch_ref[part, :].astype(F32)
        return carry

    lax.fori_loop(0, 8, widen, 0)

    def extract(slot):
        for block in range(blocks):
            number = slot * blocks + block
            planes[number] = wide[pl.ds(number, tracks, stride=stride), :].astype(BF16)

    extract(0)

    ent = ent_ref[...]
    owner = ent >> track_shift
    lane_e = iota((1, entries), 1)
    block_e = (lane_e >> beam_shift) & (blocks - 1)
    code = ((ent & (tracks - 1)) + block_e * tracks + 1).astype(F32)
    before = jnp.where(iota((entries, entries), 0) < iota((entries, entries), 1), 1.0, 0.0).astype(BF16)
    mine = jnp.where(owner == me, 1.0, 0.0)
    rank = dot_nn(mine.astype(BF16), before)
    slot_number = iota((capacity, entries), 0).astype(F32)

    def hits_of(flags, ranks, group):
        keep = flags[group : group + 1, :]
        return jnp.where(ranks[group : group + 1, :] == slot_number, keep, 0.0)

    sends = [hits_of(mine, rank, group) for group in range(groups)]
    picks = jnp.concatenate(
        [
            jnp.sum(sends[group] * code[group : group + 1, :], axis=1, keepdims=True)
            for group in range(groups)
        ],
        axis=0,
    ).astype(jnp.int32) - 1
    track_lane = iota((groups * capacity, tracks), 1)
    gathered = None
    for block in range(blocks):
        one_hot = jnp.where(picks - block * tracks == track_lane, 1.0, 0.0).astype(BF16)
        part = dot_nn(one_hot, planes[block])
        gathered = part if gathered is None else gathered + part
    for group in range(groups):
        out_rows[group] = gathered[group * capacity : (group + 1) * capacity].astype(BF16)

    pl.semaphore_wait(barrier, groups - 1 + rb_groups - 1)

    row_copies = []
    for offset in range(1, groups):
        dst = lax.rem(me + offset, groups)
        copy = user_copy(out_rows.at[dst], in_rows.at[me], row_send, row_recv, offset)
        copy.start()
        row_copies.append(copy)
    in_rows[pl.ds(me, 1)] = out_rows[pl.ds(me, 1)]

    for slot in range(1, slots):
        extract(slot)

    is_me = iota(ent.shape, 0) == me
    my_owner = jnp.sum(jnp.where(is_me, owner.astype(F32), 0.0), axis=0, keepdims=True)
    from_src = jnp.where(my_owner == iota(ent.shape, 0).astype(F32), 1.0, 0.0)
    src_rank = dot_nn(from_src.astype(BF16), before)
    arrivals = jnp.concatenate(
        [hits_of(from_src, src_rank, group) for group in range(groups)], axis=0
    )
    place = jnp.transpose(arrivals).astype(BF16)

    for copy in row_copies:
        copy.wait_recv()
    came = jnp.concatenate([in_rows[group].astype(F32) for group in range(groups)], axis=0)
    sched = dot_nn(place, came.astype(BF16))
    sched_b = sched.astype(BF16)
    turned_b = turn(sched).astype(BF16)

    full_r = dot_nt(sched_b, sched_b)
    full_i = dot_nt(sched_b, turned_b)
    shape = (beams, entries)
    lane_problem = iota(shape, 1) >> beam_shift
    gram_r = gram_i = jnp.zeros(shape, F32)
    for problem in range(cell_dev * blocks):
        part = slice(problem * beams, (problem + 1) * beams)
        here = lane_problem == problem
        gram_r = gram_r + jnp.where(here, full_r[part, :], 0.0)
        gram_i = gram_i + jnp.where(here, full_i[part, :], 0.0)
    reg_lanes = jnp.zeros((1, entries), F32)
    cell_lanes = blocks * beams
    for cell in range(cell_dev):
        reg_lanes = jnp.where(lane_e >= cell * cell_lanes, reg_ref[cell], reg_lanes)
    inv_r, inv_i = newton_inverse(gram_r, gram_i, reg_lanes, beams)

    problems = cell_dev * blocks
    square = (entries, entries)
    same = (iota(square, 0) >> beam_shift) == (iota(square, 1) >> beam_shift)
    wide_r = jnp.where(same, jnp.concatenate([inv_r] * problems, axis=0), 0.0)
    wide_i = jnp.where(same, jnp.concatenate([inv_i] * problems, axis=0), 0.0)
    vectors = dot_split(wide_r, sched_b) + dot_split(wide_i, turned_b)

    squares = vectors * vectors
    sums = [
        jnp.sum(squares[cell * cell_lanes : (cell + 1) * cell_lanes], axis=0, keepdims=True)
        for cell in range(cell_dev)
    ]
    pw_own[...] = jnp.concatenate(sums + [jnp.zeros((8 - cell_dev, width), F32)], axis=0)
    pw_copies = []
    for offset in range(1, rb_groups):
        copy = pltpu.make_async_remote_copy(
            src_ref=pw_own,
            dst_ref=pw_in.at[my_rb],
            send_sem=pw_send.at[offset],
            recv_sem=pw_recv.at[offset],
            device_id={"rb": lax.rem(my_rb + offset, rb_groups)},
            device_id_type=pl.DeviceIdType.MESH,
        )
        copy.start()
        pw_copies.append(copy)
    pw_in[pl.ds(my_rb, 1)] = pw_own[...][None]
    for copy in pw_copies:
        copy.wait_recv()
    total = jnp.sum(jnp.sum(pw_in[...], axis=0), axis=1, keepdims=True)
    scale = lax.rsqrt(total / (blocks * rb_groups) + 1e-06)
    scaled = jnp.concatenate(
        [
            vectors[cell * cell_lanes : (cell + 1) * cell_lanes] * scale[cell : cell + 1, :]
            for cell in range(cell_dev)
        ],
        axis=0,
    )
    prec = scaled.astype(BF16)
    own_w[...] = prec
    w_copies = []
    for offset in range(1, groups):
        copy = user_copy(own_w, all_w.at[me], w_send, w_recv, offset)
        copy.start()
        w_copies.append(copy)
    all_w[pl.ds(me, 1)] = prec[None]
    prec_ref[...] = prec

    prec_turned = turn(prec.astype(F32)).astype(BF16)
    z_r = dot_nt(prec, sched_b)
    z_i = dot_nt(prec_turned, sched_b)
    magnitude = jnp.where(same, z_r * z_r + z_i * z_i, 0.0)
    on_diagonal = iota(square, 0) == iota(square, 1)
    signal = jnp.sum(jnp.where(on_diagonal, magnitude, 0.0), axis=0, keepdims=True)
    leakage = jnp.sum(jnp.where(on_diagonal, 0.0, magnitude), axis=0, keepdims=True)

    for copy in w_copies:
        copy.wait_recv()

    count = cells * beams
    cell_shift = log2_of(cells)
    new_row = iota((count, count), 0)
    old_row = ((new_row & (cells - 1)) << beam_shift) + (new_row >> cell_shift)
    order = jnp.where(old_row == iota((count, count), 1), 1.0, 0.0).astype(BF16)
    for block in range(blocks):
        stacked = jnp.concatenate(
            [
                all_w[
                    group,
                    cell * cell_lanes + block * beams : cell * cell_lanes + (block + 1) * beams,
                    :,
                ]
                for group in range(groups)
                for cell in range(cell_dev)
            ],
            axis=0,
        )
        ordered = dot_nn(order, stacked)
        forms[block, 0:count, :] = ordered.astype(BF16)
        forms[block, count : 2 * count, :] = turn(ordered).astype(BF16)

    cell_row = iota((cells, tracks), 0)

    def track_powers(number, carry):
        slot, block = number // blocks, number % blocks
        projected = dot_nt(forms[block], planes[number])
        energy = jnp.sum((projected * projected).reshape(2 * beams, cells, tracks), axis=0)
        heard = cells_ref[slot]
        received[number] = jnp.sum(
            jnp.where(cell_row == heard, energy, 0.0), axis=0, keepdims=True
        )
        return carry

    lax.fori_loop(0, slots * blocks, track_powers, 0)

    floor = jnp.zeros((1, tracks), F32)
    serving = cells_ref[0]
    for cell in range(cells):
        floor = jnp.where(serving == cell, noise_ref[cell], floor)
    denominators = []
    for block in range(blocks):
        interference = received[blocks + block]
        for slot in range(2, slots):
            interference = interference + received[slot * blocks + block]
        denominators.append(interference + floor)
    power = jnp.concatenate([received[block] for block in range(blocks)], axis=0)
    all_denominators = jnp.concatenate(denominators, axis=0)

    found = jnp.zeros((groups * capacity, tracks), F32)
    for block in range(blocks):
        found = jnp.where(picks - block * tracks == track_lane, denominators[block], found)
    column = jnp.sum(found, axis=1, keepdims=True)
    dn_own[...] = jnp.concatenate(
        [
            jnp.sum(
                sends[group] * column[group * capacity : (group + 1) * capacity],
                axis=0,
                keepdims=True,
            )
            for group in range(groups)
        ],
        axis=0,
    )
    dn_copies = []
    for offset in range(1, groups):
        copy = user_copy(dn_own, dn_in.at[me], dn_send, dn_recv, offset)
        copy.start()
        dn_copies.append(copy)
    dn_in[pl.ds(me, 1)] = dn_own[...][None]

    metric_ref[...] = jnp.log2(1.0 + power / all_denominators)

    for copy in dn_copies:
        copy.wait_recv()
    every = jnp.sum(dn_in[...], axis=0)
    entry_denominator = jnp.sum(jnp.where(is_me, every, 0.0), axis=0, keepdims=True)
    rate_ref[...] = jnp.log2(1.0 + signal / (leakage + entry_denominator))

    for copy in row_copies + pw_copies + w_copies + dn_copies:
        copy.wait_send()


def on_device(channel, serving, interferers, plan, regularizer, noise_floor):
    tracks, blocks, slots, width = channel.shape
    cells, _, beams = plan.shape
    cell_dev = regularizer.shape[0]
    groups = lax.axis_size("users")
    rb_groups = lax.axis_size("rb")
    entries = cell_dev * blocks * beams
    capacity = 2 * entries // groups
    dims = (groups, rb_groups, tracks, blocks, slots, cells, beams, cell_dev, capacity)
    rows = channel.transpose(0, 2, 1, 3).reshape(tracks * slots * blocks, width)
    heard = jnp.concatenate([serving[None, :], interferers.T], axis=0)[:, None, :]
    vmem = pl.BlockSpec(memory_space=pltpu.VMEM)
    smem = pl.BlockSpec(memory_space=pltpu.SMEM)
    dma = pltpu.SemaphoreType.DMA
    precoders, metric, rate = pl.pallas_call(
        functools.partial(kernel, dims),
        out_shape=(
            jax.ShapeDtypeStruct((entries, width), BF16),
            jax.ShapeDtypeStruct((blocks, tracks), F32),
            jax.ShapeDtypeStruct((1, entries), F32),
        ),
        in_specs=[vmem, vmem, vmem, smem, smem],
        out_specs=(vmem, vmem, vmem),
        scratch_shapes=[
            pltpu.VMEM((tracks * slots * blocks, width), F32),
            pltpu.VMEM((slots * blocks, tracks, width), BF16),
            pltpu.VMEM((groups, capacity, width), BF16),
            pltpu.VMEM((groups, capacity, width), BF16),
            pltpu.VMEM((entries, width), BF16),
            pltpu.VMEM((groups, entries, width), BF16),
            pltpu.VMEM((blocks, 2 * cells * beams, width), BF16),
            pltpu.VMEM((slots * blocks, 1, tracks), F32),
            pltpu.VMEM((8, width), F32),
            pltpu.VMEM((rb_groups, 8, width), F32),
            pltpu.VMEM((groups, entries), F32),
            pltpu.VMEM((groups, groups, entries), F32),
            dma((groups,)),
            dma((groups,)),
            dma((groups,)),
            dma((groups,)),
            dma((rb_groups,)),
            dma((rb_groups,)),
            dma((groups,)),
            dma((groups,)),
        ],
        compiler_params=pltpu.CompilerParams(
            collective_id=0, has_side_effects=True, vmem_limit_bytes=48 << 20
        ),
    )(rows, plan.reshape(groups, entries), heard, regularizer, noise_floor)
    return (
        precoders.reshape(cell_dev, blocks, beams, width),
        metric.T,
        rate.reshape(cell_dev, blocks, beams),
    )


def solution(mesh):
    return jax.shard_map(
        on_device,
        mesh=mesh,
        in_specs=(
            P("users", "rb", None, None),
            P("users"),
            P("users", None),
            P(None, "rb", None),
            P("users"),
            P(),
        ),
        out_specs=(P("users", "rb", None, None), P("users", "rb"), P("users", "rb", None)),
        check_vma=False,
    )
```

```python
import functools

import jax
import jax.numpy as jnp
from jax import lax
from jax.experimental import pallas as pl
from jax.experimental.pallas import tpu as pltpu
from jax.sharding import PartitionSpec as P

ITERS = 12
F32 = jnp.float32
BF16 = jnp.bfloat16
HIGH = lax.Precision.HIGHEST


def iota(shape, dim):
    return lax.broadcasted_iota(jnp.int32, shape, dim)


def log2_of(n):
    assert n & (n - 1) == 0
    return n.bit_length() - 1


def turn(rows):
    half = rows.shape[-1] // 2
    sign = jnp.where(iota(rows.shape, 1) < half, 1.0, -1.0)
    return pltpu.roll(rows, half, 1) * sign


def dot_nt(a, b):
    return lax.dot_general(a, b, (((1,), (1,)), ((), ())), preferred_element_type=F32)


def dot_nn(a, b):
    return jnp.dot(a, b, preferred_element_type=F32)


def split3(x):
    high = x.astype(BF16)
    rest = x - high.astype(F32)
    middle = rest.astype(BF16)
    return high, middle, (rest - middle.astype(F32)).astype(BF16)


def dot_split(x, b):
    high, middle, low = split3(x)
    return dot_nn(low, b) + dot_nn(middle, b) + dot_nn(high, b)


def spread(a, beams):
    lane = iota(a.shape, 1)
    base = lane - (lane & (beams - 1))
    return lambda m: jnp.take_along_axis(a, base + m, axis=1, mode="promise_in_bounds")


def complex_product(left_r, left_i, right_r, right_i, beams):
    out_r = out_i = None
    for m in range(beams):
        lr, li = left_r(m), left_i(m)
        rr, ri = right_r[m : m + 1, :], right_i[m : m + 1, :]
        term_r = lr * rr - li * ri
        term_i = lr * ri + li * rr
        out_r = term_r if out_r is None else out_r + term_r
        out_i = term_i if out_i is None else out_i + term_i
    return out_r, out_i


def newton_inverse(gram_r, gram_i, reg_lanes, beams):
    shape = gram_r.shape
    lanes = shape[1]
    shift = log2_of(beams)
    diagonal = (iota(shape, 1) & (beams - 1)) == iota(shape, 0)
    gram_r = gram_r + jnp.where(diagonal, reg_lanes, 0.0)
    diag_row = jnp.sum(jnp.where(diagonal, gram_r, 0.0), axis=0, keepdims=True)
    same = (iota((lanes, lanes), 0) >> shift) == (iota((lanes, lanes), 1) >> shift)
    trace = jnp.dot(
        jnp.broadcast_to(diag_row, (8, lanes)),
        jnp.where(same, 1.0, 0.0),
        precision=HIGH,
        preferred_element_type=F32,
    )[0:1, :]
    start_r = jnp.where(diagonal, 1.0 / trace, 0.0)
    start_i = jnp.zeros(shape, F32)
    gather_r, gather_i = spread(gram_r, beams), spread(gram_i, beams)
    held_r = [gather_r(m) for m in range(beams)]
    held_i = [gather_i(m) for m in range(beams)]

    def step(_, carry):
        xr, xi = carry
        yr, yi = complex_product(lambda m: held_r[m], lambda m: held_i[m], xr, xi, beams)
        zr, zi = complex_product(spread(xr, beams), spread(xi, beams), yr, yi, beams)
        return 2.0 * xr - zr, 2.0 * xi - zi

    return lax.fori_loop(0, ITERS, step, (start_r, start_i))


def flip(index, mask, count):
    result = 0
    bit = 1
    while bit < count:
        digit = lax.rem(lax.div(index, bit), 2)
        result = result + bit * (1 - digit if mask & bit else digit)
        bit *= 2
    return result


def kernel(
    dims,
    ch_hbm,
    plan_hbm,
    serving_hbm,
    inter_hbm,
    reg_hbm,
    noise_hbm,
    prec_out,
    metric_out,
    rate_out,
    prec_ref,
    metric_ref,
    rate_ref,
    raw,
    plan_ref,
    inter_ref,
    cells_ref,
    reg_ref,
    noise_ref,
    wide,
    planes,
    out_rows,
    in_rows,
    own_w,
    all_w,
    forms,
    received,
    pw_own,
    pw_in,
    sc_own,
    sc_in,
    dn_own,
    dn_in,
    load_sem,
    small_sem,
    store_sem,
    row_send,
    row_recv,
    w_send,
    w_recv,
    pw_send,
    pw_recv,
    sc_send,
    sc_recv,
    dn_send,
    dn_recv,
):
    groups, rb_groups, tracks, blocks, slots, cells, beams, cell_dev, capacity = dims
    entries = cell_dev * blocks * beams
    width = raw.shape[1]
    track_shift = log2_of(tracks)
    beam_shift = log2_of(beams)
    me = lax.axis_index("users")
    my_rb = lax.axis_index("rb")

    rows = raw.shape[0]
    pieces = load_sem.shape[0]
    chunk = rows // pieces
    loads = []
    small = [
        pltpu.make_async_copy(plan_hbm, plan_ref, small_sem.at[0]),
        pltpu.make_async_copy(serving_hbm, cells_ref.at[0], small_sem.at[1]),
        pltpu.make_async_copy(inter_hbm, inter_ref, small_sem.at[2]),
        pltpu.make_async_copy(reg_hbm, reg_ref, small_sem.at[3]),
        pltpu.make_async_copy(noise_hbm, noise_ref, small_sem.at[4]),
    ]
    for copy in small:
        copy.start()
    for i in range(pieces):
        part = pl.ds(i * chunk, chunk)
        copy = pltpu.make_async_copy(ch_hbm.at[part], raw.at[part], load_sem.at[i])
        copy.start()
        loads.append(copy)

    barrier = pltpu.get_barrier_semaphore()
    for offset in range(1, groups):
        pl.semaphore_signal(
            barrier, inc=1, device_id={"users": flip(me, offset, groups)},
            device_id_type=pl.DeviceIdType.MESH,
        )
    for offset in range(1, rb_groups):
        pl.semaphore_signal(
            barrier, inc=1, device_id={"rb": flip(my_rb, offset, rb_groups)},
            device_id_type=pl.DeviceIdType.MESH,
        )

    def user_copy(src, dst, send, recv, offset):
        return pltpu.make_async_remote_copy(
            src_ref=src,
            dst_ref=dst,
            send_sem=send.at[offset],
            recv_sem=recv.at[offset],
            device_id={"users": flip(me, offset, groups)},
            device_id_type=pl.DeviceIdType.MESH,
        )

    for copy in small:
        copy.wait()
    for slot in range(1, slots):
        cells_ref[slot] = inter_ref[slot - 1 : slot, :]
    cell_lanes = blocks * beams
    spread_plan = None
    for block in range(blocks):
        lane = iota((beams, entries), 1) & (cell_lanes - 1)
        put = jnp.where(lane == iota((beams, entries), 0) + block * beams, 1.0, 0.0)
        part = jnp.dot(
            plan_ref[:, block, :].astype(F32), put, precision=HIGH, preferred_element_type=F32
        )
        spread_plan = part if spread_plan is None else spread_plan + part
    ent_f = jnp.zeros((groups, entries), F32)
    for cell in range(cell_dev):
        pick = jnp.where(
            iota((groups, cells), 1) == cell_dev * iota((groups, cells), 0) + cell, 1.0, 0.0
        )
        lane = iota((cells, entries), 1)
        in_cell = (lane >= cell * cell_lanes) & (lane < (cell + 1) * cell_lanes)
        ent_f = ent_f + jnp.dot(
            pick, jnp.where(in_cell, spread_plan, 0.0), precision=HIGH, preferred_element_type=F32
        )
    ent = ent_f.astype(jnp.int32)

    owner = ent >> track_shift
    lane_e = iota((1, entries), 1)
    block_e = (lane_e >> beam_shift) & (blocks - 1)
    code = ((ent & (tracks - 1)) + block_e * tracks + 1).astype(F32)
    before = jnp.where(
        iota((entries, entries), 0) < iota((entries, entries), 1), 1.0, 0.0
    ).astype(BF16)
    mine = jnp.where(owner == me, 1.0, 0.0)
    rank = dot_nn(mine.astype(BF16), before)
    slot_number = iota((capacity, entries), 0).astype(F32)

    def hits_of(flags, ranks, group):
        keep = flags[group : group + 1, :]
        return jnp.where(ranks[group : group + 1, :] == slot_number, keep, 0.0)

    sends = [hits_of(mine, rank, group) for group in range(groups)]
    picks = jnp.concatenate(
        [
            jnp.sum(sends[group] * code[group : group + 1, :], axis=1, keepdims=True)
            for group in range(groups)
        ],
        axis=0,
    ).astype(jnp.int32) - 1

    stride = slots * blocks
    for i in range(pieces):
        loads[i].wait()
        part = slice(i * chunk, (i + 1) * chunk)
        wide[part, :] = raw[part, :].astype(F32)

    def extract(slot):
        for block in range(blocks):
            number = slot * blocks + block
            planes[number] = wide[pl.ds(number, tracks, stride=stride), :].astype(BF16)

    extract(0)

    track_lane = iota((groups * capacity, tracks), 1)
    gathered = None
    for block in range(blocks):
        one_hot = jnp.where(picks - block * tracks == track_lane, 1.0, 0.0).astype(BF16)
        part = dot_nn(one_hot, planes[block])
        gathered = part if gathered is None else gathered + part
    for group in range(groups):
        out_rows[group] = gathered[group * capacity : (group + 1) * capacity].astype(BF16)

    pl.semaphore_wait(barrier, groups - 1 + rb_groups - 1)

    row_copies = []
    for offset in range(1, groups):
        dst = flip(me, offset, groups)
        copy = user_copy(out_rows.at[dst], in_rows.at[me], row_send, row_recv, offset)
        copy.start()
        row_copies.append(copy)
    in_rows[pl.ds(me, 1)] = out_rows[pl.ds(me, 1)]

    for slot in range(1, slots):
        extract(slot)

    is_me = iota(ent.shape, 0) == me
    my_owner = jnp.sum(jnp.where(is_me, owner.astype(F32), 0.0), axis=0, keepdims=True)
    from_src = jnp.where(my_owner == iota(ent.shape, 0).astype(F32), 1.0, 0.0)
    src_rank = dot_nn(from_src.astype(BF16), before)
    arrivals = jnp.concatenate(
        [hits_of(from_src, src_rank, group) for group in range(groups)], axis=0
    )
    place = jnp.transpose(arrivals).astype(BF16)

    for copy in row_copies:
        copy.wait_recv()
    came = jnp.concatenate([in_rows[group].astype(F32) for group in range(groups)], axis=0)
    sched = dot_nn(place, came.astype(BF16))
    sched_b = sched.astype(BF16)
    turned_b = turn(sched).astype(BF16)

    full_r = dot_nt(sched_b, sched_b)
    full_i = dot_nt(sched_b, turned_b)
    shape = (beams, entries)
    lane_problem = iota(shape, 1) >> beam_shift
    gram_r = gram_i = jnp.zeros(shape, F32)
    for problem in range(cell_dev * blocks):
        part = slice(problem * beams, (problem + 1) * beams)
        here = lane_problem == problem
        gram_r = gram_r + jnp.where(here, full_r[part, :], 0.0)
        gram_i = gram_i + jnp.where(here, full_i[part, :], 0.0)
    reg_lanes = jnp.zeros((1, entries), F32)
    for cell in range(cell_dev):
        reg_lanes = jnp.where(lane_e >= cell * cell_lanes, reg_ref[cell], reg_lanes)
    inv_r, inv_i = newton_inverse(gram_r, gram_i, reg_lanes, beams)

    problems = cell_dev * blocks
    square = (entries, entries)
    same = (iota(square, 0) >> beam_shift) == (iota(square, 1) >> beam_shift)
    wide_r = jnp.where(same, jnp.concatenate([inv_r] * problems, axis=0), 0.0)
    wide_i = jnp.where(same, jnp.concatenate([inv_i] * problems, axis=0), 0.0)
    vectors = dot_split(wide_r, sched_b) + dot_split(wide_i, turned_b)

    unscaled = vectors.astype(BF16)
    own_w[...] = unscaled
    w_copies = []
    for offset in range(1, groups):
        copy = user_copy(own_w, all_w.at[me], w_send, w_recv, offset)
        copy.start()
        w_copies.append(copy)
    all_w[pl.ds(me, 1)] = unscaled[None]

    squares = vectors * vectors
    sums = [
        jnp.sum(squares[cell * cell_lanes : (cell + 1) * cell_lanes], axis=0, keepdims=True)
        for cell in range(cell_dev)
    ]
    pw_own[...] = jnp.concatenate(sums + [jnp.zeros((8 - cell_dev, width), F32)], axis=0)
    pw_copies = []
    for offset in range(1, rb_groups):
        copy = pltpu.make_async_remote_copy(
            src_ref=pw_own,
            dst_ref=pw_in.at[my_rb],
            send_sem=pw_send.at[offset],
            recv_sem=pw_recv.at[offset],
            device_id={"rb": flip(my_rb, offset, rb_groups)},
            device_id_type=pl.DeviceIdType.MESH,
        )
        copy.start()
        pw_copies.append(copy)
    pw_in[pl.ds(my_rb, 1)] = pw_own[...][None]
    for copy in pw_copies:
        copy.wait_recv()
    total = jnp.sum(jnp.sum(pw_in[...], axis=0), axis=1, keepdims=True)
    scale = lax.rsqrt(total / (blocks * rb_groups) + 1e-06)
    sc_own[...] = jnp.broadcast_to(scale * scale, (8, width))
    sc_copies = []
    for offset in range(1, groups):
        copy = user_copy(sc_own, sc_in.at[me], sc_send, sc_recv, offset)
        copy.start()
        sc_copies.append(copy)
    sc_in[pl.ds(me, 1)] = sc_own[...][None]
    prec = jnp.concatenate(
        [
            vectors[cell * cell_lanes : (cell + 1) * cell_lanes] * scale[cell : cell + 1, :]
            for cell in range(cell_dev)
        ],
        axis=0,
    ).astype(BF16)
    prec_ref[...] = prec
    stores = [pltpu.make_async_copy(prec_ref, prec_out, store_sem.at[0])]
    stores[0].start()

    prec_turned = turn(prec.astype(F32)).astype(BF16)
    z_r = dot_nt(prec, sched_b)
    z_i = dot_nt(prec_turned, sched_b)
    magnitude = jnp.where(same, z_r * z_r + z_i * z_i, 0.0)
    on_diagonal = iota(square, 0) == iota(square, 1)
    signal = jnp.sum(jnp.where(on_diagonal, magnitude, 0.0), axis=0, keepdims=True)
    leakage = jnp.sum(jnp.where(on_diagonal, 0.0, magnitude), axis=0, keepdims=True)

    half = groups // 2
    near = lax.div(me, half)
    half_cells = half * cell_dev
    count = half_cells * beams
    cell_shift = log2_of(half_cells)
    new_row = iota((count, count), 0)
    old_row = ((new_row & (half_cells - 1)) << beam_shift) + (new_row >> cell_shift)
    order = jnp.where(old_row == iota((count, count), 1), 1.0, 0.0).astype(BF16)
    cell_row = iota((half_cells, tracks), 0)
    for turn_number in range(2):
        for offset in range(1, groups):
            if offset // half == turn_number:
                w_copies[offset - 1].wait_recv()
        first_group = half * (near if turn_number == 0 else 1 - near)
        for block in range(blocks):
            stacked = jnp.concatenate(
                [
                    all_w[
                        first_group + group,
                        cell * cell_lanes + block * beams : cell * cell_lanes + (block + 1) * beams,
                        :,
                    ]
                    for group in range(half)
                    for cell in range(cell_dev)
                ],
                axis=0,
            )
            ordered = dot_nn(order, stacked)
            forms[block, 0:count, :] = ordered.astype(BF16)
            forms[block, count : 2 * count, :] = turn(ordered).astype(BF16)

        def track_powers(number, carry, first_cell=first_group * cell_dev, keep=turn_number):
            slot, block = lax.div(number, blocks), lax.rem(number, blocks)
            projected = dot_nt(forms[block], planes[number])
            energy = jnp.sum(
                (projected * projected).reshape(2 * beams, half_cells, tracks), axis=0
            )
            heard = cells_ref[slot] - first_cell
            part = jnp.sum(jnp.where(cell_row == heard, energy, 0.0), axis=0, keepdims=True)
            received[number] = received[number] + part if keep else part
            return carry

        lax.fori_loop(0, slots * blocks, track_powers, 0)

    for copy in sc_copies:
        copy.wait_recv()
    scales = []
    for slot in range(slots):
        heard = cells_ref[slot]
        row = jnp.zeros((1, tracks), F32)
        for group in range(groups):
            for cell in range(cell_dev):
                one = sc_in[group, cell : cell + 1, 0:1]
                row = jnp.where(heard == group * cell_dev + cell, one, row)
        scales.append(row)
    floor = jnp.zeros((1, tracks), F32)
    serving = cells_ref[0]
    for cell in range(cells):
        floor = jnp.where(serving == cell, noise_ref[cell], floor)
    denominators = []
    for block in range(blocks):
        interference = received[blocks + block] * scales[1]
        for slot in range(2, slots):
            interference = interference + received[slot * blocks + block] * scales[slot]
        denominators.append(interference + floor)

    found = jnp.zeros((groups * capacity, tracks), F32)
    for block in range(blocks):
        found = jnp.where(picks - block * tracks == track_lane, denominators[block], found)
    column = jnp.sum(found, axis=1, keepdims=True)
    dn_own[...] = jnp.concatenate(
        [
            jnp.sum(
                sends[group] * column[group * capacity : (group + 1) * capacity],
                axis=0,
                keepdims=True,
            )
            for group in range(groups)
        ],
        axis=0,
    )
    dn_copies = []
    for offset in range(1, groups):
        copy = user_copy(dn_own, dn_in.at[me], dn_send, dn_recv, offset)
        copy.start()
        dn_copies.append(copy)
    dn_in[pl.ds(me, 1)] = dn_own[...][None]

    power = jnp.concatenate([received[block] * scales[0] for block in range(blocks)], axis=0)
    all_denominators = jnp.concatenate(denominators, axis=0)
    metric_ref[...] = jnp.log2(1.0 + power / all_denominators)
    stores.append(pltpu.make_async_copy(metric_ref, metric_out, store_sem.at[1]))
    stores[1].start()

    for copy in row_copies + pw_copies + w_copies + sc_copies:
        copy.wait_send()
    for copy in dn_copies:
        copy.wait_recv()
    every = jnp.sum(dn_in[...], axis=0)
    entry_denominator = jnp.sum(jnp.where(is_me, every, 0.0), axis=0, keepdims=True)
    rate = jnp.log2(1.0 + signal / (leakage + entry_denominator))
    for cell in range(cell_dev):
        for block in range(blocks):
            start = (cell * blocks + block) * beams
            rate_ref[cell, block : block + 1, :] = rate[:, start : start + beams]
    stores.append(pltpu.make_async_copy(rate_ref, rate_out, store_sem.at[2]))
    stores[2].start()
    for copy in dn_copies:
        copy.wait_send()
    for copy in stores:
        copy.wait()


def hand_over(*refs):
    count = len(refs) // 2
    copies = [
        pltpu.make_async_copy(refs[i], refs[count + i], refs[2 * count].at[i])
        for i in range(count)
    ]
    for copy in copies:
        copy.start()
    for copy in copies:
        copy.wait()


def on_device(channel, serving, interferers, plan, regularizer, noise_floor):
    tracks, blocks, slots, width = channel.shape
    cells, _, beams = plan.shape
    cell_dev = regularizer.shape[0]
    groups = lax.axis_size("users")
    rb_groups = lax.axis_size("rb")
    entries = cell_dev * blocks * beams
    capacity = 2 * entries // groups
    dims = (groups, rb_groups, tracks, blocks, slots, cells, beams, cell_dev, capacity)
    row_count = tracks * slots * blocks
    rows = channel.transpose(0, 2, 1, 3).reshape(row_count, width)
    hbm = pl.BlockSpec(memory_space=pltpu.HBM)
    dma = pltpu.SemaphoreType.DMA
    results = (
        jax.ShapeDtypeStruct((entries, width), BF16),
        jax.ShapeDtypeStruct((blocks, tracks), F32),
        jax.ShapeDtypeStruct((cell_dev, blocks, beams), F32),
    )
    made = pl.pallas_call(
        functools.partial(kernel, dims),
        out_shape=results,
        in_specs=[hbm] * 6,
        out_specs=(hbm, hbm, hbm),
        scratch_shapes=[
            *[pltpu.VMEM(result.shape, result.dtype) for result in results],
            pltpu.VMEM((row_count, width), BF16),
            pltpu.VMEM((cells, blocks, beams), jnp.int32),
            pltpu.VMEM((slots - 1, tracks), jnp.int32),
            pltpu.VMEM((slots, 1, tracks), jnp.int32),
            pltpu.SMEM(regularizer.shape, F32),
            pltpu.SMEM(noise_floor.shape, F32),
            pltpu.VMEM((row_count, width), F32),
            pltpu.VMEM((slots * blocks, tracks, width), BF16),
            pltpu.VMEM((groups, capacity, width), BF16),
            pltpu.VMEM((groups, capacity, width), BF16),
            pltpu.VMEM((entries, width), BF16),
            pltpu.VMEM((groups, entries, width), BF16),
            pltpu.VMEM((blocks, cells * beams, width), BF16),
            pltpu.VMEM((slots * blocks, 1, tracks), F32),
            pltpu.VMEM((8, width), F32),
            pltpu.VMEM((rb_groups, 8, width), F32),
            pltpu.VMEM((8, width), F32),
            pltpu.VMEM((groups, 8, width), F32),
            pltpu.VMEM((groups, entries), F32),
            pltpu.VMEM((groups, groups, entries), F32),
            dma((8,)),
            dma((5,)),
            dma((3,)),
            dma((groups,)),
            dma((groups,)),
            dma((groups,)),
            dma((groups,)),
            dma((rb_groups,)),
            dma((rb_groups,)),
            dma((groups,)),
            dma((groups,)),
            dma((groups,)),
            dma((groups,)),
        ],
        compiler_params=pltpu.CompilerParams(
            collective_id=0, has_side_effects=True, vmem_limit_bytes=64 << 20
        ),
    )(rows, plan, serving[None, :], interferers.T, regularizer, noise_floor)
    precoders, metric, rate = pl.pallas_call(
        hand_over,
        out_shape=results,
        in_specs=[hbm] * 3,
        out_specs=(hbm, hbm, hbm),
        scratch_shapes=[dma((3,))],
        compiler_params=pltpu.CompilerParams(vmem_limit_bytes=64 << 20),
    )(*made)
    return precoders.reshape(cell_dev, blocks, beams, width), metric.T, rate


def solution(mesh):
    return jax.shard_map(
        on_device,
        mesh=mesh,
        in_specs=(
            P("users", "rb", None, None),
            P("users"),
            P("users", None),
            P(None, "rb", None),
            P("users"),
            P(),
        ),
        out_specs=(P("users", "rb", None, None), P("users", "rb"), P("users", "rb", None)),
        check_vma=False,
    )
```

```python
import functools

import jax
import jax.numpy as jnp
from jax import lax
from jax.experimental import pallas as pl
from jax.experimental.pallas import tpu as pltpu
from jax.sharding import PartitionSpec as P

ITERS = 12
F32 = jnp.float32
BF16 = jnp.bfloat16
HIGH = lax.Precision.HIGHEST


def iota(shape, dim):
    return lax.broadcasted_iota(jnp.int32, shape, dim)


def log2_of(n):
    assert n & (n - 1) == 0
    return n.bit_length() - 1


def turn(rows):
    half = rows.shape[-1] // 2
    sign = jnp.where(iota(rows.shape, 1) < half, 1.0, -1.0)
    return pltpu.roll(rows, half, 1) * sign


def dot_nt(a, b):
    return lax.dot_general(a, b, (((1,), (1,)), ((), ())), preferred_element_type=F32)


def dot_nn(a, b):
    return jnp.dot(a, b, preferred_element_type=F32)


def split3(x):
    high = x.astype(BF16)
    rest = x - high.astype(F32)
    middle = rest.astype(BF16)
    return high, middle, (rest - middle.astype(F32)).astype(BF16)


def dot_split(x, b):
    high, middle, low = split3(x)
    return dot_nn(low, b) + dot_nn(middle, b) + dot_nn(high, b)


def spread(a, beams):
    lane = iota(a.shape, 1)
    base = lane - (lane & (beams - 1))
    return lambda m: jnp.take_along_axis(a, base + m, axis=1, mode="promise_in_bounds")


def complex_product(left_r, left_i, right_r, right_i, beams):
    out_r = out_i = None
    for m in range(beams):
        lr, li = left_r(m), left_i(m)
        rr, ri = right_r[m : m + 1, :], right_i[m : m + 1, :]
        term_r = lr * rr - li * ri
        term_i = lr * ri + li * rr
        out_r = term_r if out_r is None else out_r + term_r
        out_i = term_i if out_i is None else out_i + term_i
    return out_r, out_i


def newton_inverse(gram_r, gram_i, reg_lanes, beams):
    shape = gram_r.shape
    lanes = shape[1]
    shift = log2_of(beams)
    diagonal = (iota(shape, 1) & (beams - 1)) == iota(shape, 0)
    gram_r = gram_r + jnp.where(diagonal, reg_lanes, 0.0)
    diag_row = jnp.sum(jnp.where(diagonal, gram_r, 0.0), axis=0, keepdims=True)
    same = (iota((lanes, lanes), 0) >> shift) == (iota((lanes, lanes), 1) >> shift)
    trace = jnp.dot(
        jnp.broadcast_to(diag_row, (8, lanes)),
        jnp.where(same, 1.0, 0.0),
        precision=HIGH,
        preferred_element_type=F32,
    )[0:1, :]
    first = 1.0 / trace
    start_r = jnp.where(diagonal, 2.0 * first, 0.0) - gram_r * first * first
    start_i = -(gram_i * first * first)
    gather_r, gather_i = spread(gram_r, beams), spread(gram_i, beams)
    held_r = [gather_r(m) for m in range(beams)]
    held_i = [gather_i(m) for m in range(beams)]

    def step(_, carry):
        xr, xi = carry
        yr, yi = complex_product(lambda m: held_r[m], lambda m: held_i[m], xr, xi, beams)
        zr, zi = complex_product(spread(xr, beams), spread(xi, beams), yr, yi, beams)
        return 2.0 * xr - zr, 2.0 * xi - zi

    return lax.fori_loop(1, ITERS, step, (start_r, start_i))


def flip(index, mask, count):
    result = 0
    bit = 1
    while bit < count:
        digit = lax.rem(lax.div(index, bit), 2)
        result = result + bit * (1 - digit if mask & bit else digit)
        bit *= 2
    return result


def kernel(
    dims,
    ch_hbm,
    plan_hbm,
    serving_hbm,
    inter_hbm,
    reg_hbm,
    noise_hbm,
    prec_ref,
    metric_ref,
    rate_ref,
    raw,
    plan_ref,
    inter_ref,
    cells_ref,
    reg_ref,
    noise_ref,
    wide,
    planes,
    out_rows,
    in_rows,
    out_more,
    in_more,
    out_ids,
    in_ids,
    own_w,
    all_w,
    forms,
    received,
    pw_own,
    pw_in,
    sc_own,
    sc_in,
    load_sem,
    small_sem,
    row_send,
    row_recv,
    more_send,
    more_recv,
    ids_send,
    ids_recv,
    w_send,
    w_recv,
    pw_send,
    pw_recv,
    sc_send,
    sc_recv,
):
    groups, rb_groups, tracks, blocks, slots, cells, beams, cell_dev, capacity = dims
    entries = cell_dev * blocks * beams
    width = raw.shape[1]
    track_shift = log2_of(tracks)
    beam_shift = log2_of(beams)
    me = lax.axis_index("users")
    my_rb = lax.axis_index("rb")

    rows = raw.shape[0]
    pieces = load_sem.shape[0]
    chunk = rows // pieces
    loads = []
    small = [
        pltpu.make_async_copy(plan_hbm, plan_ref, small_sem.at[0]),
        pltpu.make_async_copy(serving_hbm, cells_ref.at[0], small_sem.at[1]),
        pltpu.make_async_copy(inter_hbm, inter_ref, small_sem.at[2]),
        pltpu.make_async_copy(reg_hbm, reg_ref, small_sem.at[3]),
        pltpu.make_async_copy(noise_hbm, noise_ref, small_sem.at[4]),
    ]
    for copy in small:
        copy.start()
    for i in range(pieces):
        part = pl.ds(i * chunk, chunk)
        copy = pltpu.make_async_copy(ch_hbm.at[part], raw.at[part], load_sem.at[i])
        copy.start()
        loads.append(copy)

    barrier = pltpu.get_barrier_semaphore()
    for offset in range(1, groups):
        pl.semaphore_signal(
            barrier, inc=1, device_id={"users": flip(me, offset, groups)},
            device_id_type=pl.DeviceIdType.MESH,
        )
    for offset in range(1, rb_groups):
        pl.semaphore_signal(
            barrier, inc=1, device_id={"rb": flip(my_rb, offset, rb_groups)},
            device_id_type=pl.DeviceIdType.MESH,
        )

    def user_copy(src, dst, send, recv, offset):
        return pltpu.make_async_remote_copy(
            src_ref=src,
            dst_ref=dst,
            send_sem=send.at[offset],
            recv_sem=recv.at[offset],
            device_id={"users": flip(me, offset, groups)},
            device_id_type=pl.DeviceIdType.MESH,
        )

    for copy in small:
        copy.wait()
    for slot in range(1, slots):
        cells_ref[slot] = inter_ref[slot - 1 : slot, :]
    cell_lanes = blocks * beams
    spread_plan = None
    for block in range(blocks):
        lane = iota((beams, entries), 1) & (cell_lanes - 1)
        put = jnp.where(lane == iota((beams, entries), 0) + block * beams, 1.0, 0.0)
        part = jnp.dot(
            plan_ref[:, block, :].astype(F32), put, precision=HIGH, preferred_element_type=F32
        )
        spread_plan = part if spread_plan is None else spread_plan + part
    ent_f = jnp.zeros((groups, entries), F32)
    for cell in range(cell_dev):
        pick = jnp.where(
            iota((groups, cells), 1) == cell_dev * iota((groups, cells), 0) + cell, 1.0, 0.0
        )
        lane = iota((cells, entries), 1)
        in_cell = (lane >= cell * cell_lanes) & (lane < (cell + 1) * cell_lanes)
        ent_f = ent_f + jnp.dot(
            pick, jnp.where(in_cell, spread_plan, 0.0), precision=HIGH, preferred_element_type=F32
        )
    ent = ent_f.astype(jnp.int32)

    owner = ent >> track_shift
    lane_e = iota((1, entries), 1)
    block_e = (lane_e >> beam_shift) & (blocks - 1)
    code = ((ent & (tracks - 1)) + block_e * tracks + 1).astype(F32)
    before = jnp.where(
        iota((entries, entries), 0) < iota((entries, entries), 1), 1.0, 0.0
    ).astype(BF16)
    mine = jnp.where(owner == me, 1.0, 0.0)
    rank = dot_nn(mine.astype(BF16), before)
    slot_number = iota((capacity, entries), 0).astype(F32)

    def hits_of(flags, ranks, group):
        keep = flags[group : group + 1, :]
        return jnp.where(ranks[group : group + 1, :] == slot_number, keep, 0.0)

    sends = [hits_of(mine, rank, group) for group in range(groups)]
    picks = jnp.concatenate(
        [
            jnp.sum(sends[group] * code[group : group + 1, :], axis=1, keepdims=True)
            for group in range(groups)
        ],
        axis=0,
    ).astype(jnp.int32) - 1

    stride = slots * blocks
    for i in range(pieces):
        loads[i].wait()
        part = slice(i * chunk, (i + 1) * chunk)
        wide[part, :] = raw[part, :].astype(F32)

    def extract(slot):
        for block in range(blocks):
            number = slot * blocks + block
            planes[number] = wide[pl.ds(number, tracks, stride=stride), :].astype(BF16)

    extract(0)

    track_lane = iota((groups * capacity, tracks), 1)
    gathered = None
    hots = []
    for block in range(blocks):
        hots.append(jnp.where(picks - block * tracks == track_lane, 1.0, 0.0).astype(BF16))
        part = dot_nn(hots[block], planes[block])
        gathered = part if gathered is None else gathered + part
    for group in range(groups):
        out_rows[group] = gathered[group * capacity : (group + 1) * capacity].astype(BF16)

    pl.semaphore_wait(barrier, groups - 1 + rb_groups - 1)

    row_copies = []
    for offset in range(1, groups):
        dst = flip(me, offset, groups)
        copy = user_copy(out_rows.at[dst], in_rows.at[me], row_send, row_recv, offset)
        copy.start()
        row_copies.append(copy)
    in_rows[pl.ds(me, 1)] = out_rows[pl.ds(me, 1)]

    for slot in range(1, slots):
        extract(slot)

    gathered = any_hot = None
    for block in range(blocks):
        planes_of = [planes[slot * blocks + block] for slot in range(1, slots)]
        part = dot_nn(hots[block], jnp.concatenate(planes_of, axis=1))
        gathered = part if gathered is None else gathered + part
        any_hot = hots[block] if any_hot is None else any_hot + hots[block]
    heard_rows = [cells_ref[slot].astype(F32) for slot in range(1, slots)]
    heard_rows.append(jnp.zeros((9 - slots, tracks), F32))
    ids = dot_nt(jnp.concatenate(heard_rows, axis=0).astype(BF16), any_hot)
    out_ids[...] = jnp.zeros(out_ids.shape, F32)
    for group in range(groups):
        part = slice(group * capacity, (group + 1) * capacity)
        out_more[group] = gathered[part].astype(BF16)
        out_ids[group, :, 0:capacity] = ids[:, part]
    more_copies = []
    for offset in range(1, groups):
        dst = flip(me, offset, groups)
        copy = user_copy(out_more.at[dst], in_more.at[me], more_send, more_recv, offset)
        copy.start()
        more_copies.append(copy)
        copy = user_copy(out_ids.at[dst], in_ids.at[me], ids_send, ids_recv, offset)
        copy.start()
        more_copies.append(copy)
    in_more[pl.ds(me, 1)] = out_more[pl.ds(me, 1)]
    in_ids[pl.ds(me, 1)] = out_ids[pl.ds(me, 1)]

    is_me = iota(ent.shape, 0) == me
    my_owner = jnp.sum(jnp.where(is_me, owner.astype(F32), 0.0), axis=0, keepdims=True)
    from_src = jnp.where(my_owner == iota(ent.shape, 0).astype(F32), 1.0, 0.0)
    src_rank = dot_nn(from_src.astype(BF16), before)
    arrivals = [hits_of(from_src, src_rank, group) for group in range(groups)]
    place = jnp.transpose(jnp.concatenate(arrivals, axis=0)).astype(BF16)

    for copy in row_copies:
        copy.wait_recv()
    came = jnp.concatenate([in_rows[group].astype(F32) for group in range(groups)], axis=0)
    sched = dot_nn(place, came.astype(BF16))
    sched_b = sched.astype(BF16)
    turned_b = turn(sched).astype(BF16)

    full_r = dot_nt(sched_b, sched_b)
    full_i = dot_nt(sched_b, turned_b)
    shape = (beams, entries)
    lane_problem = iota(shape, 1) >> beam_shift
    gram_r = gram_i = jnp.zeros(shape, F32)
    for problem in range(cell_dev * blocks):
        part = slice(problem * beams, (problem + 1) * beams)
        here = lane_problem == problem
        gram_r = gram_r + jnp.where(here, full_r[part, :], 0.0)
        gram_i = gram_i + jnp.where(here, full_i[part, :], 0.0)
    reg_lanes = jnp.zeros((1, entries), F32)
    for cell in range(cell_dev):
        reg_lanes = jnp.where(lane_e >= cell * cell_lanes, reg_ref[cell], reg_lanes)
    inv_r, inv_i = newton_inverse(gram_r, gram_i, reg_lanes, beams)

    problems = cell_dev * blocks
    square = (entries, entries)
    same = (iota(square, 0) >> beam_shift) == (iota(square, 1) >> beam_shift)
    wide_r = jnp.where(same, jnp.concatenate([inv_r] * problems, axis=0), 0.0)
    wide_i = jnp.where(same, jnp.concatenate([inv_i] * problems, axis=0), 0.0)
    vectors = dot_split(wide_r, sched_b) + dot_split(wide_i, turned_b)

    cell_shift = log2_of(cell_dev)
    new_row = iota(square, 0)
    old_row = (new_row & (cell_dev - 1)) * cell_lanes + (new_row >> cell_shift)
    order = jnp.where(old_row == iota(square, 1), 1.0, 0.0).astype(BF16)
    unscaled = dot_nn(order, vectors.astype(BF16)).astype(BF16)
    own_w[...] = unscaled
    w_copies = []
    for offset in range(1, groups):
        copy = user_copy(own_w, all_w.at[me], w_send, w_recv, offset)
        copy.start()
        w_copies.append(copy)
    all_w[pl.ds(me, 1)] = unscaled[None]

    squares = vectors * vectors
    sums = [
        jnp.sum(squares[cell * cell_lanes : (cell + 1) * cell_lanes], axis=0, keepdims=True)
        for cell in range(cell_dev)
    ]
    pw_own[...] = jnp.concatenate(sums + [jnp.zeros((8 - cell_dev, width), F32)], axis=0)
    pw_copies = []
    for offset in range(1, rb_groups):
        copy = pltpu.make_async_remote_copy(
            src_ref=pw_own,
            dst_ref=pw_in.at[my_rb],
            send_sem=pw_send.at[offset],
            recv_sem=pw_recv.at[offset],
            device_id={"rb": flip(my_rb, offset, rb_groups)},
            device_id_type=pl.DeviceIdType.MESH,
        )
        copy.start()
        pw_copies.append(copy)
    pw_in[pl.ds(my_rb, 1)] = pw_own[...][None]
    for copy in pw_copies:
        copy.wait_recv()
    total = jnp.sum(jnp.sum(pw_in[...], axis=0), axis=1, keepdims=True)
    scale = lax.rsqrt(total / (blocks * rb_groups) + 1e-06)
    sc_own[...] = jnp.broadcast_to(scale * scale, (8, width))
    sc_copies = []
    for offset in range(1, groups):
        copy = user_copy(sc_own, sc_in.at[me], sc_send, sc_recv, offset)
        copy.start()
        sc_copies.append(copy)
    sc_in[pl.ds(me, 1)] = sc_own[...][None]
    prec = jnp.concatenate(
        [
            vectors[cell * cell_lanes : (cell + 1) * cell_lanes] * scale[cell : cell + 1, :]
            for cell in range(cell_dev)
        ],
        axis=0,
    ).astype(BF16)
    prec_ref[...] = prec

    prec_turned = turn(prec.astype(F32)).astype(BF16)
    z_r = dot_nt(prec, sched_b)
    z_i = dot_nt(prec_turned, sched_b)
    magnitude = jnp.where(same, z_r * z_r + z_i * z_i, 0.0)
    on_diagonal = iota(square, 0) == iota(square, 1)
    signal = jnp.sum(jnp.where(on_diagonal, magnitude, 0.0), axis=0, keepdims=True)
    leakage = jnp.sum(jnp.where(on_diagonal, 0.0, magnitude), axis=0, keepdims=True)

    for copy in more_copies:
        copy.wait_recv()
    came = jnp.concatenate([in_more[group].astype(F32) for group in range(groups)], axis=0)
    more = dot_nn(place, came.astype(BF16))
    entry_rows = jnp.concatenate(
        [more[:, slot * width : (slot + 1) * width] for slot in range(slots - 1)], axis=0
    ).astype(BF16)
    entry_ids = jnp.zeros((8, entries), F32)
    for group in range(groups):
        known = in_ids[group, :, 0:capacity].astype(BF16)
        entry_ids = entry_ids + dot_nn(known, arrivals[group].astype(BF16))
    entry_heard = jnp.concatenate(
        [entry_ids[slot : slot + 1, :] for slot in range(slots - 1)], axis=1
    ).astype(jnp.int32)
    entry_lanes = (slots - 1) * entries
    entry_block = (iota((1, entry_lanes), 1) >> beam_shift) & (blocks - 1)

    half = groups // 2
    near = lax.div(me, half)
    part_rows = cell_dev * beams
    form_rows = 2 * part_rows

    def heard_power(form, rows, heard):
        lanes = rows.shape[0]
        projected = dot_nt(form, rows)
        energy = jnp.sum(
            (projected * projected).reshape(half, form_rows // 8, 8, lanes), axis=1
        )
        shape = (half, 8, lanes)
        cell = iota(shape, 0) * cell_dev + (iota(shape, 1) & (cell_dev - 1))
        found = jnp.sum(jnp.where(cell == heard[None], energy, 0.0), axis=0)
        return jnp.sum(found, axis=0, keepdims=True)

    entry_power = jnp.zeros((1, entry_lanes), F32)
    for turn_number in range(2):
        for offset in range(1, groups):
            if offset // half == turn_number:
                w_copies[offset - 1].wait_recv()
        first_group = half * (near if turn_number == 0 else 1 - near)
        first_cell = first_group * cell_dev
        for block in range(blocks):
            for group in range(half):
                rows_in = all_w[first_group + group, block * part_rows : (block + 1) * part_rows, :]
                at = group * form_rows
                forms[block, at : at + part_rows, :] = rows_in
                forms[block, at + part_rows : at + form_rows, :] = turn(
                    rows_in.astype(F32)
                ).astype(BF16)

        def track_powers(slot, carry, first_cell=first_cell, keep=turn_number):
            heard = cells_ref[slot] - first_cell
            for block in range(blocks):
                number = slot * blocks + block
                part = heard_power(forms[block], planes[number], heard)
                received[number] = received[number] + part if keep else part
            return carry

        lax.fori_loop(0, slots, track_powers, 0)
        for block in range(blocks):
            part = heard_power(forms[block], entry_rows, entry_heard - first_cell)
            entry_power = entry_power + jnp.where(entry_block == block, part, 0.0)

    for copy in sc_copies:
        copy.wait_recv()

    def scale_row(heard):
        row = jnp.zeros(heard.shape, F32)
        for group in range(groups):
            for cell in range(cell_dev):
                one = sc_in[group, cell : cell + 1, 0:1]
                row = jnp.where(heard == group * cell_dev + cell, one, row)
        return row

    entry_power = entry_power * scale_row(entry_heard)
    entry_denominator = entry_power[:, 0:entries]
    for slot in range(1, slots - 1):
        entry_denominator = entry_denominator + entry_power[:, slot * entries : (slot + 1) * entries]
    noise_lanes = jnp.zeros((1, entries), F32)
    for cell in range(cell_dev):
        noise_lanes = jnp.where(
            lane_e >= cell * cell_lanes, noise_ref[me * cell_dev + cell], noise_lanes
        )
    entry_denominator = entry_denominator + noise_lanes
    rate = jnp.log2(1.0 + signal / (leakage + entry_denominator))
    for cell in range(cell_dev):
        for block in range(blocks):
            start = (cell * blocks + block) * beams
            rate_ref[cell, block : block + 1, :] = rate[:, start : start + beams]

    scales = [scale_row(cells_ref[slot]) for slot in range(slots)]
    floor = jnp.zeros((1, tracks), F32)
    serving = cells_ref[0]
    for cell in range(cells):
        floor = jnp.where(serving == cell, noise_ref[cell], floor)
    for block in range(blocks):
        interference = received[blocks + block] * scales[1]
        for slot in range(2, slots):
            interference = interference + received[slot * blocks + block] * scales[slot]
        power = received[block] * scales[0]
        metric_ref[block : block + 1, :] = jnp.log2(1.0 + power / (interference + floor))

    for copy in row_copies + more_copies + pw_copies + w_copies + sc_copies:
        copy.wait_send()


def hand_over(*refs):
    count = len(refs) // 2
    copies = [
        pltpu.make_async_copy(refs[i], refs[count + i], refs[2 * count].at[i])
        for i in range(count)
    ]
    for copy in copies:
        copy.start()
    for copy in copies:
        copy.wait()


def on_device(channel, serving, interferers, plan, regularizer, noise_floor):
    tracks, blocks, slots, width = channel.shape
    cells, _, beams = plan.shape
    cell_dev = regularizer.shape[0]
    groups = lax.axis_size("users")
    rb_groups = lax.axis_size("rb")
    entries = cell_dev * blocks * beams
    capacity = 2 * entries // groups
    dims = (groups, rb_groups, tracks, blocks, slots, cells, beams, cell_dev, capacity)
    row_count = tracks * slots * blocks
    rows = channel.transpose(0, 2, 1, 3).reshape(row_count, width)
    hbm = pl.BlockSpec(memory_space=pltpu.HBM)
    vmem = pl.BlockSpec(memory_space=pltpu.VMEM)
    dma = pltpu.SemaphoreType.DMA
    results = (
        jax.ShapeDtypeStruct((entries, width), BF16),
        jax.ShapeDtypeStruct((blocks, tracks), F32),
        jax.ShapeDtypeStruct((cell_dev, blocks, beams), F32),
    )
    made = pl.pallas_call(
        functools.partial(kernel, dims),
        out_shape=results,
        in_specs=[hbm] * 6,
        out_specs=(vmem, vmem, vmem),
        scratch_shapes=[
            pltpu.VMEM((row_count, width), BF16),
            pltpu.VMEM((cells, blocks, beams), jnp.int32),
            pltpu.VMEM((slots - 1, tracks), jnp.int32),
            pltpu.VMEM((slots, 1, tracks), jnp.int32),
            pltpu.SMEM(regularizer.shape, F32),
            pltpu.SMEM(noise_floor.shape, F32),
            pltpu.VMEM((row_count, width), F32),
            pltpu.VMEM((slots * blocks, tracks, width), BF16),
            pltpu.VMEM((groups, capacity, width), BF16),
            pltpu.VMEM((groups, capacity, width), BF16),
            pltpu.VMEM((groups, capacity, (slots - 1) * width), BF16),
            pltpu.VMEM((groups, capacity, (slots - 1) * width), BF16),
            pltpu.VMEM((groups, 8, width), F32),
            pltpu.VMEM((groups, 8, width), F32),
            pltpu.VMEM((entries, width), BF16),
            pltpu.VMEM((groups, entries, width), BF16),
            pltpu.VMEM((blocks, cells * beams, width), BF16),
            pltpu.VMEM((slots * blocks, 1, tracks), F32),
            pltpu.VMEM((8, width), F32),
            pltpu.VMEM((rb_groups, 8, width), F32),
            pltpu.VMEM((8, width), F32),
            pltpu.VMEM((groups, 8, width), F32),
            dma((8,)),
            dma((5,)),
            *[dma((groups,)) for _ in range(8)],
            dma((rb_groups,)),
            dma((rb_groups,)),
            dma((groups,)),
            dma((groups,)),
        ],
        compiler_params=pltpu.CompilerParams(
            collective_id=0, has_side_effects=True, vmem_limit_bytes=64 << 20
        ),
    )(rows, plan, serving[None, :], interferers.T, regularizer, noise_floor)
    precoders, metric, rate = pl.pallas_call(
        hand_over,
        out_shape=results,
        in_specs=[vmem] * 3,
        out_specs=(hbm, hbm, hbm),
        scratch_shapes=[dma((3,))],
        compiler_params=pltpu.CompilerParams(vmem_limit_bytes=64 << 20),
    )(*made)
    return precoders.reshape(cell_dev, blocks, beams, width), metric.T, rate


def solution(mesh):
    return jax.shard_map(
        on_device,
        mesh=mesh,
        in_specs=(
            P("users", "rb", None, None),
            P("users"),
            P("users", None),
            P(None, "rb", None),
            P("users"),
            P(),
        ),
        out_specs=(P("users", "rb", None, None), P("users", "rb"), P("users", "rb", None)),
        check_vma=False,
    )
```

```python
import functools

import jax
import jax.numpy as jnp
from jax import lax
from jax.experimental import pallas as pl
from jax.experimental.pallas import tpu as pltpu
from jax.sharding import PartitionSpec as P

ITERS = 12
F32 = jnp.float32
BF16 = jnp.bfloat16
HIGH = lax.Precision.HIGHEST


def iota(shape, dim):
    return lax.broadcasted_iota(jnp.int32, shape, dim)


def log2_of(n):
    assert n & (n - 1) == 0
    return n.bit_length() - 1


def turn(rows):
    half = rows.shape[-1] // 2
    sign = jnp.where(iota(rows.shape, 1) < half, 1.0, -1.0)
    return pltpu.roll(rows, half, 1) * sign


def dot_nt(a, b):
    return lax.dot_general(a, b, (((1,), (1,)), ((), ())), preferred_element_type=F32)


def dot_nn(a, b):
    return jnp.dot(a, b, preferred_element_type=F32)


def dot_split(x, b):
    high = x.astype(BF16)
    rest = (x - high.astype(F32)).astype(BF16)
    return dot_nn(rest, b) + dot_nn(high, b)


def spread(a, beams):
    lane = iota(a.shape, 1)
    base = lane - (lane & (beams - 1))
    return lambda m: jnp.take_along_axis(a, base + m, axis=1, mode="promise_in_bounds")


def complex_product(left_r, left_i, right_r, right_i, beams):
    out_r = out_i = None
    for m in range(beams):
        lr, li = left_r(m), left_i(m)
        rr, ri = right_r[m : m + 1, :], right_i[m : m + 1, :]
        term_r = lr * rr - li * ri
        term_i = lr * ri + li * rr
        out_r = term_r if out_r is None else out_r + term_r
        out_i = term_i if out_i is None else out_i + term_i
    return out_r, out_i


def newton_inverse(gram_r, gram_i, reg_lanes, beams):
    shape = gram_r.shape
    lanes = shape[1]
    shift = log2_of(beams)
    diagonal = (iota(shape, 1) & (beams - 1)) == iota(shape, 0)
    gram_r = gram_r + jnp.where(diagonal, reg_lanes, 0.0)
    diag_row = jnp.sum(jnp.where(diagonal, gram_r, 0.0), axis=0, keepdims=True)
    same = (iota((lanes, lanes), 0) >> shift) == (iota((lanes, lanes), 1) >> shift)
    trace = jnp.dot(
        jnp.broadcast_to(diag_row, (8, lanes)),
        jnp.where(same, 1.0, 0.0),
        precision=HIGH,
        preferred_element_type=F32,
    )[0:1, :]
    first = 1.0 / trace
    rest_r = jnp.where(diagonal, 1.0, 0.0) - gram_r * first
    rest_i = -(gram_i * first)
    start_r = jnp.where(diagonal, first, 0.0) + rest_r * first
    start_i = rest_i * first

    def square_of(rr, ri):
        return complex_product(spread(rr, beams), spread(ri, beams), rr, ri, beams)

    def step(_, carry):
        rr, ri, xr, xi = carry
        left_r, left_i = spread(rr, beams), spread(ri, beams)
        both_r = jnp.concatenate([xr, rr], axis=1)
        both_i = jnp.concatenate([xi, ri], axis=1)
        twice_r = lambda m: jnp.concatenate([left_r(m)] * 2, axis=1)
        twice_i = lambda m: jnp.concatenate([left_i(m)] * 2, axis=1)
        zr, zi = complex_product(twice_r, twice_i, both_r, both_i, beams)
        return zr[:, lanes:], zi[:, lanes:], xr + zr[:, :lanes], xi + zi[:, :lanes]

    one_r, one_i = square_of(rest_r, rest_i)
    rr, ri, xr, xi = lax.fori_loop(1, ITERS - 1, step, (one_r, one_i, start_r, start_i))
    zr, zi = complex_product(spread(rr, beams), spread(ri, beams), xr, xi, beams)
    return xr + zr, xi + zi


def flip(index, mask, count):
    result = 0
    bit = 1
    while bit < count:
        digit = lax.rem(lax.div(index, bit), 2)
        result = result + bit * (1 - digit if mask & bit else digit)
        bit *= 2
    return result


def kernel(
    dims,
    ch_hbm,
    plan_hbm,
    serving_hbm,
    inter_hbm,
    reg_hbm,
    noise_hbm,
    prec_ref,
    metric_ref,
    rate_ref,
    raw,
    plan_ref,
    inter_ref,
    cells_ref,
    reg_ref,
    noise_ref,
    wide,
    planes,
    out_rows,
    in_rows,
    out_more,
    in_more,
    out_ids,
    in_ids,
    own_w,
    all_w,
    forms,
    received,
    pw_own,
    pw_in,
    sc_own,
    sc_in,
    load_sem,
    small_sem,
    row_send,
    row_recv,
    more_send,
    more_recv,
    ids_send,
    ids_recv,
    w_send,
    w_recv,
    pw_send,
    pw_recv,
    sc_send,
    sc_recv,
):
    groups, rb_groups, tracks, blocks, slots, cells, beams, cell_dev, capacity = dims
    entries = cell_dev * blocks * beams
    width = raw.shape[1]
    track_shift = log2_of(tracks)
    beam_shift = log2_of(beams)
    me = lax.axis_index("users")
    my_rb = lax.axis_index("rb")

    rows = raw.shape[0]
    pieces = load_sem.shape[0]
    chunk = rows // pieces
    loads = []
    small = [
        pltpu.make_async_copy(plan_hbm, plan_ref, small_sem.at[0]),
        pltpu.make_async_copy(serving_hbm, cells_ref.at[0], small_sem.at[1]),
        pltpu.make_async_copy(inter_hbm, inter_ref, small_sem.at[2]),
        pltpu.make_async_copy(reg_hbm, reg_ref, small_sem.at[3]),
        pltpu.make_async_copy(noise_hbm, noise_ref, small_sem.at[4]),
    ]
    for copy in small:
        copy.start()
    for i in range(pieces):
        part = pl.ds(i * chunk, chunk)
        copy = pltpu.make_async_copy(ch_hbm.at[part], raw.at[part], load_sem.at[i])
        copy.start()
        loads.append(copy)

    barrier = pltpu.get_barrier_semaphore()
    for offset in range(1, groups):
        pl.semaphore_signal(
            barrier, inc=1, device_id={"users": flip(me, offset, groups)},
            device_id_type=pl.DeviceIdType.MESH,
        )
    for offset in range(1, rb_groups):
        pl.semaphore_signal(
            barrier, inc=1, device_id={"rb": flip(my_rb, offset, rb_groups)},
            device_id_type=pl.DeviceIdType.MESH,
        )

    def user_copy(src, dst, send, recv, offset):
        return pltpu.make_async_remote_copy(
            src_ref=src,
            dst_ref=dst,
            send_sem=send.at[offset],
            recv_sem=recv.at[offset],
            device_id={"users": flip(me, offset, groups)},
            device_id_type=pl.DeviceIdType.MESH,
        )

    for copy in small:
        copy.wait()
    for slot in range(1, slots):
        cells_ref[slot] = inter_ref[slot - 1 : slot, :]
    cell_lanes = blocks * beams
    spread_plan = None
    for block in range(blocks):
        lane = iota((beams, entries), 1) & (cell_lanes - 1)
        put = jnp.where(lane == iota((beams, entries), 0) + block * beams, 1.0, 0.0)
        part = jnp.dot(
            plan_ref[:, block, :].astype(F32), put, precision=HIGH, preferred_element_type=F32
        )
        spread_plan = part if spread_plan is None else spread_plan + part
    ent_f = jnp.zeros((groups, entries), F32)
    for cell in range(cell_dev):
        pick = jnp.where(
            iota((groups, cells), 1) == cell_dev * iota((groups, cells), 0) + cell, 1.0, 0.0
        )
        lane = iota((cells, entries), 1)
        in_cell = (lane >= cell * cell_lanes) & (lane < (cell + 1) * cell_lanes)
        ent_f = ent_f + jnp.dot(
            pick, jnp.where(in_cell, spread_plan, 0.0), precision=HIGH, preferred_element_type=F32
        )
    ent = ent_f.astype(jnp.int32)

    owner = ent >> track_shift
    lane_e = iota((1, entries), 1)
    block_e = (lane_e >> beam_shift) & (blocks - 1)
    code = ((ent & (tracks - 1)) + block_e * tracks + 1).astype(F32)
    before = jnp.where(
        iota((entries, entries), 0) < iota((entries, entries), 1), 1.0, 0.0
    ).astype(BF16)
    mine = jnp.where(owner == me, 1.0, 0.0)
    rank = dot_nn(mine.astype(BF16), before)
    slot_number = iota((capacity, entries), 0).astype(F32)

    def hits_of(flags, ranks, group):
        keep = flags[group : group + 1, :]
        return jnp.where(ranks[group : group + 1, :] == slot_number, keep, 0.0)

    sends = [hits_of(mine, rank, group) for group in range(groups)]
    picks = jnp.concatenate(
        [
            jnp.sum(sends[group] * code[group : group + 1, :], axis=1, keepdims=True)
            for group in range(groups)
        ],
        axis=0,
    ).astype(jnp.int32) - 1

    stride = slots * blocks
    for i in range(pieces):
        loads[i].wait()
        part = slice(i * chunk, (i + 1) * chunk)
        wide[part, :] = raw[part, :].astype(F32)

    def extract(slot):
        for block in range(blocks):
            number = slot * blocks + block
            planes[number] = wide[pl.ds(number, tracks, stride=stride), :].astype(BF16)

    extract(0)

    track_lane = iota((groups * capacity, tracks), 1)
    gathered = None
    hots = []
    for block in range(blocks):
        hots.append(jnp.where(picks - block * tracks == track_lane, 1.0, 0.0).astype(BF16))
        part = dot_nn(hots[block], planes[block])
        gathered = part if gathered is None else gathered + part
    for group in range(groups):
        out_rows[group] = gathered[group * capacity : (group + 1) * capacity].astype(BF16)

    pl.semaphore_wait(barrier, groups - 1 + rb_groups - 1)

    row_copies = []
    for offset in range(1, groups):
        dst = flip(me, offset, groups)
        copy = user_copy(out_rows.at[dst], in_rows.at[me], row_send, row_recv, offset)
        copy.start()
        row_copies.append(copy)
    in_rows[pl.ds(me, 1)] = out_rows[pl.ds(me, 1)]

    for slot in range(1, slots):
        extract(slot)

    gathered = any_hot = None
    for block in range(blocks):
        planes_of = [planes[slot * blocks + block] for slot in range(1, slots)]
        part = dot_nn(hots[block], jnp.concatenate(planes_of, axis=1))
        gathered = part if gathered is None else gathered + part
        any_hot = hots[block] if any_hot is None else any_hot + hots[block]
    heard_rows = [cells_ref[slot].astype(F32) for slot in range(1, slots)]
    heard_rows.append(jnp.zeros((9 - slots, tracks), F32))
    ids = dot_nt(jnp.concatenate(heard_rows, axis=0).astype(BF16), any_hot)
    out_ids[...] = jnp.zeros(out_ids.shape, F32)
    for group in range(groups):
        part = slice(group * capacity, (group + 1) * capacity)
        out_more[group] = gathered[part].astype(BF16)
        out_ids[group, :, 0:capacity] = ids[0 : slots - 1, part]
    more_copies = []
    for offset in range(1, groups):
        dst = flip(me, offset, groups)
        copy = user_copy(out_more.at[dst], in_more.at[me], more_send, more_recv, offset)
        copy.start()
        more_copies.append(copy)
        copy = user_copy(out_ids.at[dst], in_ids.at[me], ids_send, ids_recv, offset)
        copy.start()
        more_copies.append(copy)
    in_more[pl.ds(me, 1)] = out_more[pl.ds(me, 1)]
    in_ids[pl.ds(me, 1)] = out_ids[pl.ds(me, 1)]

    is_me = iota(ent.shape, 0) == me
    my_owner = jnp.sum(jnp.where(is_me, owner.astype(F32), 0.0), axis=0, keepdims=True)
    from_src = jnp.where(my_owner == iota(ent.shape, 0).astype(F32), 1.0, 0.0)
    src_rank = dot_nn(from_src.astype(BF16), before)
    arrivals = [hits_of(from_src, src_rank, group) for group in range(groups)]
    place = jnp.transpose(jnp.concatenate(arrivals, axis=0)).astype(BF16)

    for copy in row_copies:
        copy.wait_recv()
    came = jnp.concatenate([in_rows[group].astype(F32) for group in range(groups)], axis=0)
    sched = dot_nn(place, came.astype(BF16))
    sched_b = sched.astype(BF16)
    turned_b = turn(sched).astype(BF16)

    full_r = dot_nt(sched_b, sched_b)
    full_i = dot_nt(sched_b, turned_b)
    shape = (beams, entries)
    lane_problem = iota(shape, 1) >> beam_shift
    gram_r = gram_i = jnp.zeros(shape, F32)
    for problem in range(cell_dev * blocks):
        part = slice(problem * beams, (problem + 1) * beams)
        here = lane_problem == problem
        gram_r = gram_r + jnp.where(here, full_r[part, :], 0.0)
        gram_i = gram_i + jnp.where(here, full_i[part, :], 0.0)
    reg_lanes = jnp.zeros((1, entries), F32)
    for cell in range(cell_dev):
        reg_lanes = jnp.where(lane_e >= cell * cell_lanes, reg_ref[cell], reg_lanes)
    inv_r, inv_i = newton_inverse(gram_r, gram_i, reg_lanes, beams)

    problems = cell_dev * blocks
    square = (entries, entries)
    same = (iota(square, 0) >> beam_shift) == (iota(square, 1) >> beam_shift)
    wide_r = jnp.where(same, jnp.concatenate([inv_r] * problems, axis=0), 0.0)
    wide_i = jnp.where(same, jnp.concatenate([inv_i] * problems, axis=0), 0.0)
    vectors = dot_split(
        jnp.concatenate([wide_r, wide_i], axis=1),
        jnp.concatenate([sched_b, turned_b], axis=0),
    )

    cell_shift = log2_of(cell_dev)
    new_row = iota(square, 0)
    old_row = (new_row & (cell_dev - 1)) * cell_lanes + (new_row >> cell_shift)
    order = jnp.where(old_row == iota(square, 1), 1.0, 0.0).astype(BF16)
    unscaled = dot_nn(order, vectors.astype(BF16)).astype(BF16)
    own_w[...] = unscaled
    w_copies = []
    for offset in range(1, groups):
        copy = user_copy(own_w, all_w.at[me], w_send, w_recv, offset)
        copy.start()
        w_copies.append(copy)
    all_w[pl.ds(me, 1)] = unscaled[None]

    squares = vectors * vectors
    sums = [
        jnp.sum(squares[cell * cell_lanes : (cell + 1) * cell_lanes], axis=0, keepdims=True)
        for cell in range(cell_dev)
    ]
    pw_own[...] = jnp.concatenate(sums + [jnp.zeros((8 - cell_dev, width), F32)], axis=0)
    pw_copies = []
    for offset in range(1, rb_groups):
        copy = pltpu.make_async_remote_copy(
            src_ref=pw_own,
            dst_ref=pw_in.at[my_rb],
            send_sem=pw_send.at[offset],
            recv_sem=pw_recv.at[offset],
            device_id={"rb": flip(my_rb, offset, rb_groups)},
            device_id_type=pl.DeviceIdType.MESH,
        )
        copy.start()
        pw_copies.append(copy)
    pw_in[pl.ds(my_rb, 1)] = pw_own[...][None]
    for copy in pw_copies:
        copy.wait_recv()
    total = jnp.sum(jnp.sum(pw_in[...], axis=0), axis=1, keepdims=True)
    scale = lax.rsqrt(total / (blocks * rb_groups) + 1e-06)
    sc_own[...] = jnp.broadcast_to(scale * scale, (8, width))
    sc_copies = []
    for offset in range(1, groups):
        copy = user_copy(sc_own, sc_in.at[me], sc_send, sc_recv, offset)
        copy.start()
        sc_copies.append(copy)
    sc_in[pl.ds(me, 1)] = sc_own[...][None]
    prec = jnp.concatenate(
        [
            vectors[cell * cell_lanes : (cell + 1) * cell_lanes] * scale[cell : cell + 1, :]
            for cell in range(cell_dev)
        ],
        axis=0,
    ).astype(BF16)
    prec_ref[...] = prec

    prec_turned = turn(prec.astype(F32)).astype(BF16)
    z_r = dot_nt(prec, sched_b)
    z_i = dot_nt(prec_turned, sched_b)
    magnitude = jnp.where(same, z_r * z_r + z_i * z_i, 0.0)
    on_diagonal = iota(square, 0) == iota(square, 1)
    signal = jnp.sum(jnp.where(on_diagonal, magnitude, 0.0), axis=0, keepdims=True)
    leakage = jnp.sum(jnp.where(on_diagonal, 0.0, magnitude), axis=0, keepdims=True)

    for copy in more_copies:
        copy.wait_recv()
    came = jnp.concatenate([in_more[group].astype(F32) for group in range(groups)], axis=0)
    more = dot_nn(place, came.astype(BF16))
    entry_rows = jnp.concatenate(
        [more[:, slot * width : (slot + 1) * width] for slot in range(slots - 1)], axis=0
    ).astype(BF16)
    entry_ids = jnp.zeros((slots - 1, entries), F32)
    for group in range(groups):
        known = in_ids[group, :, 0:capacity].astype(BF16)
        entry_ids = entry_ids + dot_nn(known, arrivals[group].astype(BF16))
    entry_heard = jnp.concatenate(
        [entry_ids[slot : slot + 1, :] for slot in range(slots - 1)], axis=1
    ).astype(jnp.int32)
    entry_lanes = (slots - 1) * entries
    entry_block = (iota((1, entry_lanes), 1) >> beam_shift) & (blocks - 1)

    half = groups // 2
    near = lax.div(me, half)
    part_rows = cell_dev * beams
    form_rows = 2 * part_rows

    def heard_power(form, rows, heard):
        lanes = rows.shape[0]
        projected = dot_nt(form, rows)
        energy = jnp.sum(
            (projected * projected).reshape(half, form_rows // 8, 8, lanes), axis=1
        )
        shape = (half, 8, lanes)
        cell = iota(shape, 0) * cell_dev + (iota(shape, 1) & (cell_dev - 1))
        found = jnp.sum(jnp.where(cell == heard[None], energy, 0.0), axis=0)
        return jnp.sum(found, axis=0, keepdims=True)

    entry_power = jnp.zeros((1, entry_lanes), F32)
    for turn_number in range(2):
        for offset in range(1, groups):
            if offset // half == turn_number:
                w_copies[offset - 1].wait_recv()
        first_group = half * (near if turn_number == 0 else 1 - near)
        first_cell = first_group * cell_dev
        for block in range(blocks):
            for group in range(half):
                rows_in = all_w[first_group + group, block * part_rows : (block + 1) * part_rows, :]
                at = group * form_rows
                forms[block, at : at + part_rows, :] = rows_in
                forms[block, at + part_rows : at + form_rows, :] = turn(
                    rows_in.astype(F32)
                ).astype(BF16)

        def track_powers(slot, carry, first_cell=first_cell, keep=turn_number):
            heard = cells_ref[slot] - first_cell
            for block in range(blocks):
                number = slot * blocks + block
                part = heard_power(forms[block], planes[number], heard)
                received[number] = received[number] + part if keep else part
            return carry

        lax.fori_loop(0, slots, track_powers, 0)
        for block in range(blocks):
            part = heard_power(forms[block], entry_rows, entry_heard - first_cell)
            entry_power = entry_power + jnp.where(entry_block == block, part, 0.0)

    for copy in sc_copies:
        copy.wait_recv()

    def scale_row(heard):
        row = jnp.zeros(heard.shape, F32)
        for group in range(groups):
            for cell in range(cell_dev):
                one = sc_in[group, cell : cell + 1, 0:1]
                row = jnp.where(heard == group * cell_dev + cell, one, row)
        return row

    entry_power = entry_power * scale_row(entry_heard)
    entry_denominator = entry_power[:, 0:entries]
    for slot in range(1, slots - 1):
        entry_denominator = entry_denominator + entry_power[:, slot * entries : (slot + 1) * entries]
    noise_lanes = jnp.zeros((1, entries), F32)
    for cell in range(cell_dev):
        noise_lanes = jnp.where(
            lane_e >= cell * cell_lanes, noise_ref[me * cell_dev + cell], noise_lanes
        )
    entry_denominator = entry_denominator + noise_lanes
    rate = jnp.log2(1.0 + signal / (leakage + entry_denominator))
    for cell in range(cell_dev):
        for block in range(blocks):
            start = (cell * blocks + block) * beams
            rate_ref[cell, block : block + 1, :] = rate[:, start : start + beams]

    scales = [scale_row(cells_ref[slot]) for slot in range(slots)]
    floor = jnp.zeros((1, tracks), F32)
    serving = cells_ref[0]
    for cell in range(cells):
        floor = jnp.where(serving == cell, noise_ref[cell], floor)
    for block in range(blocks):
        interference = received[blocks + block] * scales[1]
        for slot in range(2, slots):
            interference = interference + received[slot * blocks + block] * scales[slot]
        power = received[block] * scales[0]
        metric_ref[block : block + 1, :] = jnp.log2(1.0 + power / (interference + floor))

    for copy in row_copies + more_copies + pw_copies + w_copies + sc_copies:
        copy.wait_send()


def hand_over(*refs):
    count = len(refs) // 2
    copies = [
        pltpu.make_async_copy(refs[i], refs[count + i], refs[2 * count].at[i])
        for i in range(count)
    ]
    for copy in copies:
        copy.start()
    for copy in copies:
        copy.wait()


def on_device(channel, serving, interferers, plan, regularizer, noise_floor):
    tracks, blocks, slots, width = channel.shape
    cells, _, beams = plan.shape
    cell_dev = regularizer.shape[0]
    groups = lax.axis_size("users")
    rb_groups = lax.axis_size("rb")
    entries = cell_dev * blocks * beams
    capacity = 2 * entries // groups
    dims = (groups, rb_groups, tracks, blocks, slots, cells, beams, cell_dev, capacity)
    row_count = tracks * slots * blocks
    rows = channel.transpose(0, 2, 1, 3).reshape(row_count, width)
    hbm = pl.BlockSpec(memory_space=pltpu.HBM)
    vmem = pl.BlockSpec(memory_space=pltpu.VMEM)
    dma = pltpu.SemaphoreType.DMA
    results = (
        jax.ShapeDtypeStruct((entries, width), BF16),
        jax.ShapeDtypeStruct((blocks, tracks), F32),
        jax.ShapeDtypeStruct((cell_dev, blocks, beams), F32),
    )
    made = pl.pallas_call(
        functools.partial(kernel, dims),
        out_shape=results,
        in_specs=[hbm] * 6,
        out_specs=(vmem, vmem, vmem),
        scratch_shapes=[
            pltpu.VMEM((row_count, width), BF16),
            pltpu.VMEM((cells, blocks, beams), jnp.int32),
            pltpu.VMEM((slots - 1, tracks), jnp.int32),
            pltpu.VMEM((slots, 1, tracks), jnp.int32),
            pltpu.SMEM(regularizer.shape, F32),
            pltpu.SMEM(noise_floor.shape, F32),
            pltpu.VMEM((row_count, width), F32),
            pltpu.VMEM((slots * blocks, tracks, width), BF16),
            pltpu.VMEM((groups, capacity, width), BF16),
            pltpu.VMEM((groups, capacity, width), BF16),
            pltpu.VMEM((groups, capacity, (slots - 1) * width), BF16),
            pltpu.VMEM((groups, capacity, (slots - 1) * width), BF16),
            pltpu.VMEM((groups, slots - 1, width), F32),
            pltpu.VMEM((groups, slots - 1, width), F32),
            pltpu.VMEM((entries, width), BF16),
            pltpu.VMEM((groups, entries, width), BF16),
            pltpu.VMEM((blocks, cells * beams, width), BF16),
            pltpu.VMEM((slots * blocks, 1, tracks), F32),
            pltpu.VMEM((8, width), F32),
            pltpu.VMEM((rb_groups, 8, width), F32),
            pltpu.VMEM((8, width), F32),
            pltpu.VMEM((groups, 8, width), F32),
            dma((8,)),
            dma((5,)),
            *[dma((groups,)) for _ in range(8)],
            dma((rb_groups,)),
            dma((rb_groups,)),
            dma((groups,)),
            dma((groups,)),
        ],
        compiler_params=pltpu.CompilerParams(
            collective_id=0, has_side_effects=True, vmem_limit_bytes=64 << 20
        ),
    )(rows, plan, serving[None, :], interferers.T, regularizer, noise_floor)
    precoders, metric, rate = pl.pallas_call(
        hand_over,
        out_shape=results,
        in_specs=[vmem] * 3,
        out_specs=(hbm, hbm, hbm),
        scratch_shapes=[dma((3,))],
        compiler_params=pltpu.CompilerParams(vmem_limit_bytes=64 << 20),
    )(*made)
    return precoders.reshape(cell_dev, blocks, beams, width), metric.T, rate


def solution(mesh):
    return jax.shard_map(
        on_device,
        mesh=mesh,
        in_specs=(
            P("users", "rb", None, None),
            P("users"),
            P("users", None),
            P(None, "rb", None),
            P("users"),
            P(),
        ),
        out_specs=(P("users", "rb", None, None), P("users", "rb"), P("users", "rb", None)),
        check_vma=False,
    )
```

```python
import functools

import jax
import jax.numpy as jnp
from jax import lax
from jax.experimental import pallas as pl
from jax.experimental.pallas import tpu as pltpu
from jax.sharding import PartitionSpec as P

ITERS = 12
F32 = jnp.float32
BF16 = jnp.bfloat16
HIGH = lax.Precision.HIGHEST


def iota(shape, dim):
    return lax.broadcasted_iota(jnp.int32, shape, dim)


def log2_of(n):
    assert n & (n - 1) == 0
    return n.bit_length() - 1


def turn(rows):
    half = rows.shape[-1] // 2
    sign = jnp.where(iota(rows.shape, 1) < half, 1.0, -1.0)
    return pltpu.roll(rows, half, 1) * sign


def dot_nt(a, b):
    return lax.dot_general(a, b, (((1,), (1,)), ((), ())), preferred_element_type=F32)


def dot_nn(a, b):
    return jnp.dot(a, b, preferred_element_type=F32)


def split3(x):
    high = x.astype(BF16)
    rest = x - high.astype(F32)
    middle = rest.astype(BF16)
    return high, middle, (rest - middle.astype(F32)).astype(BF16)


def dot_split(x, b):
    high, middle, low = split3(x)
    return dot_nn(low, b) + dot_nn(middle, b) + dot_nn(high, b)


def spread(a, beams):
    lane = iota(a.shape, 1)
    base = lane - (lane & (beams - 1))
    return lambda m: jnp.take_along_axis(a, base + m, axis=1, mode="promise_in_bounds")


def complex_product(left_r, left_i, right_r, right_i, beams):
    out_r = out_i = None
    for m in range(beams):
        lr, li = left_r(m), left_i(m)
        rr, ri = right_r[m : m + 1, :], right_i[m : m + 1, :]
        term_r = lr * rr - li * ri
        term_i = lr * ri + li * rr
        out_r = term_r if out_r is None else out_r + term_r
        out_i = term_i if out_i is None else out_i + term_i
    return out_r, out_i


def newton_inverse(gram_r, gram_i, reg_lanes, beams):
    shape = gram_r.shape
    lanes = shape[1]
    shift = log2_of(beams)
    diagonal = (iota(shape, 1) & (beams - 1)) == iota(shape, 0)
    gram_r = gram_r + jnp.where(diagonal, reg_lanes, 0.0)
    diag_row = jnp.sum(jnp.where(diagonal, gram_r, 0.0), axis=0, keepdims=True)
    same = (iota((lanes, lanes), 0) >> shift) == (iota((lanes, lanes), 1) >> shift)
    trace = jnp.dot(
        jnp.broadcast_to(diag_row, (8, lanes)),
        jnp.where(same, 1.0, 0.0),
        precision=HIGH,
        preferred_element_type=F32,
    )[0:1, :]
    first = 1.0 / trace
    start_r = jnp.where(diagonal, 2.0 * first, 0.0) - gram_r * first * first
    start_i = -(gram_i * first * first)
    gather_r, gather_i = spread(gram_r, beams), spread(gram_i, beams)
    held_r = [gather_r(m) for m in range(beams)]
    held_i = [gather_i(m) for m in range(beams)]

    def step(_, carry):
        xr, xi = carry
        yr, yi = complex_product(lambda m: held_r[m], lambda m: held_i[m], xr, xi, beams)
        zr, zi = complex_product(spread(xr, beams), spread(xi, beams), yr, yi, beams)
        return 2.0 * xr - zr, 2.0 * xi - zi

    return lax.fori_loop(1, ITERS, step, (start_r, start_i))


def flip(index, mask, count):
    result = 0
    bit = 1
    while bit < count:
        digit = lax.rem(lax.div(index, bit), 2)
        result = result + bit * (1 - digit if mask & bit else digit)
        bit *= 2
    return result


def kernel(
    dims,
    ch_hbm,
    plan_hbm,
    serving_hbm,
    inter_hbm,
    reg_hbm,
    noise_hbm,
    prec_ref,
    metric_ref,
    rate_ref,
    raw,
    plan_ref,
    inter_ref,
    cells_ref,
    reg_ref,
    noise_ref,
    wide,
    planes,
    out_rows,
    in_rows,
    out_more,
    in_more,
    out_ids,
    in_ids,
    own_w,
    all_w,
    forms,
    received,
    pw_own,
    pw_in,
    sc_own,
    sc_in,
    load_sem,
    small_sem,
    row_send,
    row_recv,
    more_send,
    more_recv,
    ids_send,
    ids_recv,
    w_send,
    w_recv,
    pw_send,
    pw_recv,
    sc_send,
    sc_recv,
):
    groups, rb_groups, tracks, blocks, slots, cells, beams, cell_dev, capacity = dims
    entries = cell_dev * blocks * beams
    width = raw.shape[1]
    track_shift = log2_of(tracks)
    beam_shift = log2_of(beams)
    me = lax.axis_index("users")
    my_rb = lax.axis_index("rb")

    rows = raw.shape[0]
    pieces = load_sem.shape[0]
    chunk = rows // pieces
    loads = []
    small = [
        pltpu.make_async_copy(plan_hbm, plan_ref, small_sem.at[0]),
        pltpu.make_async_copy(serving_hbm, cells_ref.at[0], small_sem.at[1]),
        pltpu.make_async_copy(inter_hbm, inter_ref, small_sem.at[2]),
        pltpu.make_async_copy(reg_hbm, reg_ref, small_sem.at[3]),
        pltpu.make_async_copy(noise_hbm, noise_ref, small_sem.at[4]),
    ]
    for copy in small:
        copy.start()
    for i in range(pieces):
        part = pl.ds(i * chunk, chunk)
        copy = pltpu.make_async_copy(ch_hbm.at[part], raw.at[part], load_sem.at[i])
        copy.start()
        loads.append(copy)

    barrier = pltpu.get_barrier_semaphore()
    for offset in range(1, groups):
        pl.semaphore_signal(
            barrier, inc=1, device_id={"users": flip(me, offset, groups)},
            device_id_type=pl.DeviceIdType.MESH,
        )
    for offset in range(1, rb_groups):
        pl.semaphore_signal(
            barrier, inc=1, device_id={"rb": flip(my_rb, offset, rb_groups)},
            device_id_type=pl.DeviceIdType.MESH,
        )

    def user_copy(src, dst, send, recv, offset):
        return pltpu.make_async_remote_copy(
            src_ref=src,
            dst_ref=dst,
            send_sem=send.at[offset],
            recv_sem=recv.at[offset],
            device_id={"users": flip(me, offset, groups)},
            device_id_type=pl.DeviceIdType.MESH,
        )

    for copy in small:
        copy.wait()
    for slot in range(1, slots):
        cells_ref[slot] = inter_ref[slot - 1 : slot, :]
    cell_lanes = blocks * beams
    spread_plan = None
    for block in range(blocks):
        lane = iota((beams, entries), 1) & (cell_lanes - 1)
        put = jnp.where(lane == iota((beams, entries), 0) + block * beams, 1.0, 0.0)
        part = jnp.dot(
            plan_ref[:, block, :].astype(F32), put, precision=HIGH, preferred_element_type=F32
        )
        spread_plan = part if spread_plan is None else spread_plan + part
    ent_f = jnp.zeros((groups, entries), F32)
    for cell in range(cell_dev):
        pick = jnp.where(
            iota((groups, cells), 1) == cell_dev * iota((groups, cells), 0) + cell, 1.0, 0.0
        )
        lane = iota((cells, entries), 1)
        in_cell = (lane >= cell * cell_lanes) & (lane < (cell + 1) * cell_lanes)
        ent_f = ent_f + jnp.dot(
            pick, jnp.where(in_cell, spread_plan, 0.0), precision=HIGH, preferred_element_type=F32
        )
    ent = ent_f.astype(jnp.int32)

    owner = ent >> track_shift
    lane_e = iota((1, entries), 1)
    block_e = (lane_e >> beam_shift) & (blocks - 1)
    code = ((ent & (tracks - 1)) + block_e * tracks + 1).astype(F32)
    before = jnp.where(
        iota((entries, entries), 0) < iota((entries, entries), 1), 1.0, 0.0
    ).astype(BF16)
    mine = jnp.where(owner == me, 1.0, 0.0)
    rank = dot_nn(mine.astype(BF16), before)
    slot_number = iota((capacity, entries), 0).astype(F32)

    def hits_of(flags, ranks, group):
        keep = flags[group : group + 1, :]
        return jnp.where(ranks[group : group + 1, :] == slot_number, keep, 0.0)

    sends = [hits_of(mine, rank, group) for group in range(groups)]
    picks = jnp.concatenate(
        [
            jnp.sum(sends[group] * code[group : group + 1, :], axis=1, keepdims=True)
            for group in range(groups)
        ],
        axis=0,
    ).astype(jnp.int32) - 1

    stride = slots * blocks
    for i in range(pieces):
        loads[i].wait()
        part = slice(i * chunk, (i + 1) * chunk)
        wide[part, :] = raw[part, :].astype(F32)

    def extract(slot):
        for block in range(blocks):
            number = slot * blocks + block
            planes[number] = wide[pl.ds(number, tracks, stride=stride), :].astype(BF16)

    extract(0)

    track_lane = iota((groups * capacity, tracks), 1)
    gathered = None
    hots = []
    for block in range(blocks):
        hots.append(jnp.where(picks - block * tracks == track_lane, 1.0, 0.0).astype(BF16))
        part = dot_nn(hots[block], planes[block])
        gathered = part if gathered is None else gathered + part
    for group in range(groups):
        out_rows[group] = gathered[group * capacity : (group + 1) * capacity].astype(BF16)

    pl.semaphore_wait(barrier, groups - 1 + rb_groups - 1)

    row_copies = []
    for offset in range(1, groups):
        dst = flip(me, offset, groups)
        copy = user_copy(out_rows.at[dst], in_rows.at[me], row_send, row_recv, offset)
        copy.start()
        row_copies.append(copy)
    in_rows[pl.ds(me, 1)] = out_rows[pl.ds(me, 1)]

    for slot in range(1, slots):
        extract(slot)

    gathered = any_hot = None
    for block in range(blocks):
        planes_of = [planes[slot * blocks + block] for slot in range(1, slots)]
        part = dot_nn(hots[block], jnp.concatenate(planes_of, axis=1))
        gathered = part if gathered is None else gathered + part
        any_hot = hots[block] if any_hot is None else any_hot + hots[block]
    heard_rows = [cells_ref[slot].astype(F32) for slot in range(1, slots)]
    heard_rows.append(jnp.zeros((9 - slots, tracks), F32))
    ids = dot_nt(jnp.concatenate(heard_rows, axis=0).astype(BF16), any_hot)
    out_ids[...] = jnp.zeros(out_ids.shape, F32)
    for group in range(groups):
        part = slice(group * capacity, (group + 1) * capacity)
        out_more[group] = gathered[part].astype(BF16)
        out_ids[group, :, 0:capacity] = ids[0 : slots - 1, part]
    more_copies = []
    for offset in range(1, groups):
        dst = flip(me, offset, groups)
        copy = user_copy(out_more.at[dst], in_more.at[me], more_send, more_recv, offset)
        copy.start()
        more_copies.append(copy)
        copy = user_copy(out_ids.at[dst], in_ids.at[me], ids_send, ids_recv, offset)
        copy.start()
        more_copies.append(copy)
    in_more[pl.ds(me, 1)] = out_more[pl.ds(me, 1)]
    in_ids[pl.ds(me, 1)] = out_ids[pl.ds(me, 1)]

    is_me = iota(ent.shape, 0) == me
    my_owner = jnp.sum(jnp.where(is_me, owner.astype(F32), 0.0), axis=0, keepdims=True)
    from_src = jnp.where(my_owner == iota(ent.shape, 0).astype(F32), 1.0, 0.0)
    src_rank = dot_nn(from_src.astype(BF16), before)
    arrivals = [hits_of(from_src, src_rank, group) for group in range(groups)]
    place = jnp.transpose(jnp.concatenate(arrivals, axis=0)).astype(BF16)

    for copy in row_copies:
        copy.wait_recv()
    came = jnp.concatenate([in_rows[group].astype(F32) for group in range(groups)], axis=0)
    sched = dot_nn(place, came.astype(BF16))
    sched_b = sched.astype(BF16)
    turned_b = turn(sched).astype(BF16)

    full_r = dot_nt(sched_b, sched_b)
    full_i = dot_nt(sched_b, turned_b)
    shape = (beams, entries)
    lane_problem = iota(shape, 1) >> beam_shift
    gram_r = gram_i = jnp.zeros(shape, F32)
    for problem in range(cell_dev * blocks):
        part = slice(problem * beams, (problem + 1) * beams)
        here = lane_problem == problem
        gram_r = gram_r + jnp.where(here, full_r[part, :], 0.0)
        gram_i = gram_i + jnp.where(here, full_i[part, :], 0.0)
    reg_lanes = jnp.zeros((1, entries), F32)
    for cell in range(cell_dev):
        reg_lanes = jnp.where(lane_e >= cell * cell_lanes, reg_ref[cell], reg_lanes)
    inv_r, inv_i = newton_inverse(gram_r, gram_i, reg_lanes, beams)

    problems = cell_dev * blocks
    square = (entries, entries)
    same = (iota(square, 0) >> beam_shift) == (iota(square, 1) >> beam_shift)
    wide_r = jnp.where(same, jnp.concatenate([inv_r] * problems, axis=0), 0.0)
    wide_i = jnp.where(same, jnp.concatenate([inv_i] * problems, axis=0), 0.0)
    vectors = dot_split(wide_r, sched_b) + dot_split(wide_i, turned_b)

    cell_shift = log2_of(cell_dev)
    new_row = iota(square, 0)
    old_row = (new_row & (cell_dev - 1)) * cell_lanes + (new_row >> cell_shift)
    order = jnp.where(old_row == iota(square, 1), 1.0, 0.0).astype(BF16)
    unscaled = dot_nn(order, vectors.astype(BF16)).astype(BF16)
    own_w[...] = unscaled
    half = groups // 2
    w_copies = {}
    for offset in range(1, groups):
        if offset < half or offset % 2 == 0:
            w_copies[offset] = user_copy(own_w, all_w.at[me], w_send, w_recv, offset)
            w_copies[offset].start()
    all_w[pl.ds(me, 1)] = unscaled[None]

    squares = vectors * vectors
    sums = [
        jnp.sum(squares[cell * cell_lanes : (cell + 1) * cell_lanes], axis=0, keepdims=True)
        for cell in range(cell_dev)
    ]
    pw_own[...] = jnp.concatenate(sums + [jnp.zeros((8 - cell_dev, width), F32)], axis=0)
    pw_copies = []
    for offset in range(1, rb_groups):
        copy = pltpu.make_async_remote_copy(
            src_ref=pw_own,
            dst_ref=pw_in.at[my_rb],
            send_sem=pw_send.at[offset],
            recv_sem=pw_recv.at[offset],
            device_id={"rb": flip(my_rb, offset, rb_groups)},
            device_id_type=pl.DeviceIdType.MESH,
        )
        copy.start()
        pw_copies.append(copy)
    pw_in[pl.ds(my_rb, 1)] = pw_own[...][None]
    for copy in pw_copies:
        copy.wait_recv()
    total = jnp.sum(jnp.sum(pw_in[...], axis=0), axis=1, keepdims=True)
    scale = lax.rsqrt(total / (blocks * rb_groups) + 1e-06)
    sc_own[...] = jnp.broadcast_to(scale * scale, (8, width))
    sc_copies = []
    for offset in range(1, groups):
        copy = user_copy(sc_own, sc_in.at[me], sc_send, sc_recv, offset)
        copy.start()
        sc_copies.append(copy)
    sc_in[pl.ds(me, 1)] = sc_own[...][None]
    prec = jnp.concatenate(
        [
            vectors[cell * cell_lanes : (cell + 1) * cell_lanes] * scale[cell : cell + 1, :]
            for cell in range(cell_dev)
        ],
        axis=0,
    ).astype(BF16)
    prec_ref[...] = prec

    prec_turned = turn(prec.astype(F32)).astype(BF16)
    z_r = dot_nt(prec, sched_b)
    z_i = dot_nt(prec_turned, sched_b)
    magnitude = jnp.where(same, z_r * z_r + z_i * z_i, 0.0)
    on_diagonal = iota(square, 0) == iota(square, 1)
    signal = jnp.sum(jnp.where(on_diagonal, magnitude, 0.0), axis=0, keepdims=True)
    leakage = jnp.sum(jnp.where(on_diagonal, 0.0, magnitude), axis=0, keepdims=True)

    for copy in more_copies:
        copy.wait_recv()
    came = jnp.concatenate([in_more[group].astype(F32) for group in range(groups)], axis=0)
    more = dot_nn(place, came.astype(BF16))
    entry_rows = jnp.concatenate(
        [more[:, slot * width : (slot + 1) * width] for slot in range(slots - 1)], axis=0
    ).astype(BF16)
    entry_ids = jnp.zeros((slots - 1, entries), F32)
    for group in range(groups):
        known = in_ids[group, :, 0:capacity].astype(BF16)
        entry_ids = entry_ids + dot_nn(known, arrivals[group].astype(BF16))
    entry_heard = jnp.concatenate(
        [entry_ids[slot : slot + 1, :] for slot in range(slots - 1)], axis=1
    ).astype(jnp.int32)
    entry_lanes = (slots - 1) * entries
    entry_block = (iota((1, entry_lanes), 1) >> beam_shift) & (blocks - 1)

    near = lax.div(me, half)
    parity = lax.rem(me, 2)
    part_rows = cell_dev * beams
    form_rows = 2 * part_rows

    def heard_power(form, rows, heard, count, step):
        lanes = rows.shape[0]
        projected = dot_nt(form, rows)
        energy = jnp.sum(
            (projected * projected).reshape(count, form_rows // 8, 8, lanes), axis=1
        )
        shape = (count, 8, lanes)
        cell = iota(shape, 0) * (step * cell_dev) + (iota(shape, 1) & (cell_dev - 1))
        found = jnp.sum(jnp.where(cell == heard[None], energy, 0.0), axis=0)
        return jnp.sum(found, axis=0, keepdims=True)

    def hand_on():
        for offset in range(half, groups, 2):
            w_copies[offset].wait_recv()
            source = flip(me, offset, groups)
            relay = pltpu.make_async_remote_copy(
                src_ref=all_w.at[source],
                dst_ref=all_w.at[source],
                send_sem=w_send.at[offset + 1],
                recv_sem=w_recv.at[offset + 1],
                device_id={"users": flip(me, 1, groups)},
                device_id_type=pl.DeviceIdType.MESH,
            )
            relay.start()
            w_copies[offset + 1] = relay

    def add_powers(first_group, count, step, keep, middle):
        first_cell = first_group * cell_dev
        size = count * form_rows
        for block in range(blocks):
            for number in range(count):
                rows_in = all_w[
                    first_group + step * number, block * part_rows : (block + 1) * part_rows, :
                ]
                at = number * form_rows
                forms[block, at : at + part_rows, :] = rows_in
                forms[block, at + part_rows : at + form_rows, :] = turn(
                    rows_in.astype(F32)
                ).astype(BF16)

        def track_powers(slot, carry):
            heard = cells_ref[slot] - first_cell
            for block in range(blocks):
                number = slot * blocks + block
                part = heard_power(forms[block, 0:size], planes[number], heard, count, step)
                received[number] = received[number] + part if keep else part
            return carry

        if middle is None:
            lax.fori_loop(0, slots, track_powers, 0)
        else:
            lax.fori_loop(0, slots - 1, track_powers, 0)
            middle()
            track_powers(slots - 1, 0)
        total = jnp.zeros((1, entry_lanes), F32)
        for block in range(blocks):
            part = heard_power(forms[block, 0:size], entry_rows, entry_heard - first_cell, count, step)
            total = total + jnp.where(entry_block == block, part, 0.0)
        return total

    far = half * (1 - near)
    for offset in range(1, half):
        w_copies[offset].wait_recv()
    entry_power = add_powers(half * near, half, 1, False, hand_on)
    entry_power = entry_power + add_powers(far + parity, half // 2, 2, True, None)
    for offset in range(half + 1, groups, 2):
        w_copies[offset].wait_recv()
    entry_power = entry_power + add_powers(far + 1 - parity, half // 2, 2, True, None)

    for copy in sc_copies:
        copy.wait_recv()

    def scale_row(heard):
        row = jnp.zeros(heard.shape, F32)
        for group in range(groups):
            for cell in range(cell_dev):
                one = sc_in[group, cell : cell + 1, 0:1]
                row = jnp.where(heard == group * cell_dev + cell, one, row)
        return row

    entry_power = entry_power * scale_row(entry_heard)
    entry_denominator = entry_power[:, 0:entries]
    for slot in range(1, slots - 1):
        entry_denominator = entry_denominator + entry_power[:, slot * entries : (slot + 1) * entries]
    noise_lanes = jnp.zeros((1, entries), F32)
    for cell in range(cell_dev):
        noise_lanes = jnp.where(
            lane_e >= cell * cell_lanes, noise_ref[me * cell_dev + cell], noise_lanes
        )
    entry_denominator = entry_denominator + noise_lanes
    rate = jnp.log2(1.0 + signal / (leakage + entry_denominator))
    for cell in range(cell_dev):
        for block in range(blocks):
            start = (cell * blocks + block) * beams
            rate_ref[cell, block : block + 1, :] = rate[:, start : start + beams]

    scales = [scale_row(cells_ref[slot]) for slot in range(slots)]
    floor = jnp.zeros((1, tracks), F32)
    serving = cells_ref[0]
    for cell in range(cells):
        floor = jnp.where(serving == cell, noise_ref[cell], floor)
    for block in range(blocks):
        interference = received[blocks + block] * scales[1]
        for slot in range(2, slots):
            interference = interference + received[slot * blocks + block] * scales[slot]
        power = received[block] * scales[0]
        metric_ref[block : block + 1, :] = jnp.log2(1.0 + power / (interference + floor))

    for copy in row_copies + more_copies + pw_copies + list(w_copies.values()) + sc_copies:
        copy.wait_send()


def hand_over(*refs):
    count = len(refs) // 2
    copies = [
        pltpu.make_async_copy(refs[i], refs[count + i], refs[2 * count].at[i])
        for i in range(count)
    ]
    for copy in copies:
        copy.start()
    for copy in copies:
        copy.wait()


def on_device(channel, serving, interferers, plan, regularizer, noise_floor):
    tracks, blocks, slots, width = channel.shape
    cells, _, beams = plan.shape
    cell_dev = regularizer.shape[0]
    groups = lax.axis_size("users")
    rb_groups = lax.axis_size("rb")
    entries = cell_dev * blocks * beams
    capacity = 2 * entries // groups
    dims = (groups, rb_groups, tracks, blocks, slots, cells, beams, cell_dev, capacity)
    row_count = tracks * slots * blocks
    rows = channel.transpose(0, 2, 1, 3).reshape(row_count, width)
    hbm = pl.BlockSpec(memory_space=pltpu.HBM)
    vmem = pl.BlockSpec(memory_space=pltpu.VMEM)
    dma = pltpu.SemaphoreType.DMA
    results = (
        jax.ShapeDtypeStruct((entries, width), BF16),
        jax.ShapeDtypeStruct((blocks, tracks), F32),
        jax.ShapeDtypeStruct((cell_dev, blocks, beams), F32),
    )
    made = pl.pallas_call(
        functools.partial(kernel, dims),
        out_shape=results,
        in_specs=[hbm] * 6,
        out_specs=(vmem, vmem, vmem),
        scratch_shapes=[
            pltpu.VMEM((row_count, width), BF16),
            pltpu.VMEM((cells, blocks, beams), jnp.int32),
            pltpu.VMEM((slots - 1, tracks), jnp.int32),
            pltpu.VMEM((slots, 1, tracks), jnp.int32),
            pltpu.SMEM(regularizer.shape, F32),
            pltpu.SMEM(noise_floor.shape, F32),
            pltpu.VMEM((row_count, width), F32),
            pltpu.VMEM((slots * blocks, tracks, width), BF16),
            pltpu.VMEM((groups, capacity, width), BF16),
            pltpu.VMEM((groups, capacity, width), BF16),
            pltpu.VMEM((groups, capacity, (slots - 1) * width), BF16),
            pltpu.VMEM((groups, capacity, (slots - 1) * width), BF16),
            pltpu.VMEM((groups, slots - 1, width), F32),
            pltpu.VMEM((groups, slots - 1, width), F32),
            pltpu.VMEM((entries, width), BF16),
            pltpu.VMEM((groups, entries, width), BF16),
            pltpu.VMEM((blocks, cells * beams, width), BF16),
            pltpu.VMEM((slots * blocks, 1, tracks), F32),
            pltpu.VMEM((8, width), F32),
            pltpu.VMEM((rb_groups, 8, width), F32),
            pltpu.VMEM((8, width), F32),
            pltpu.VMEM((groups, 8, width), F32),
            dma((8,)),
            dma((5,)),
            *[dma((groups,)) for _ in range(8)],
            dma((rb_groups,)),
            dma((rb_groups,)),
            dma((groups,)),
            dma((groups,)),
        ],
        compiler_params=pltpu.CompilerParams(
            collective_id=0, has_side_effects=True, vmem_limit_bytes=64 << 20
        ),
    )(rows, plan, serving[None, :], interferers.T, regularizer, noise_floor)
    precoders, metric, rate = pl.pallas_call(
        hand_over,
        out_shape=results,
        in_specs=[vmem] * 3,
        out_specs=(hbm, hbm, hbm),
        scratch_shapes=[dma((3,))],
        compiler_params=pltpu.CompilerParams(vmem_limit_bytes=64 << 20),
    )(*made)
    return precoders.reshape(cell_dev, blocks, beams, width), metric.T, rate


def solution(mesh):
    return jax.shard_map(
        on_device,
        mesh=mesh,
        in_specs=(
            P("users", "rb", None, None),
            P("users"),
            P("users", None),
            P(None, "rb", None),
            P("users"),
            P(),
        ),
        out_specs=(P("users", "rb", None, None), P("users", "rb"), P("users", "rb", None)),
        check_vma=False,
    )
```

```python
import functools

import jax
import jax.numpy as jnp
from jax import lax
from jax.experimental import pallas as pl
from jax.experimental.pallas import tpu as pltpu
from jax.sharding import PartitionSpec as P

ITERS = 12
F32 = jnp.float32
BF16 = jnp.bfloat16
HIGH = lax.Precision.HIGHEST


def iota(shape, dim):
    return lax.broadcasted_iota(jnp.int32, shape, dim)


def log2_of(n):
    assert n & (n - 1) == 0
    return n.bit_length() - 1


def turn(rows):
    half = rows.shape[-1] // 2
    sign = jnp.where(iota(rows.shape, 1) < half, 1.0, -1.0)
    return pltpu.roll(rows, half, 1) * sign


def dot_nt(a, b):
    return lax.dot_general(a, b, (((1,), (1,)), ((), ())), preferred_element_type=F32)


def dot_nn(a, b):
    return jnp.dot(a, b, preferred_element_type=F32)


def split3(x):
    high = x.astype(BF16)
    rest = x - high.astype(F32)
    middle = rest.astype(BF16)
    return high, middle, (rest - middle.astype(F32)).astype(BF16)


def dot_split(x, b):
    high, middle, low = split3(x)
    return dot_nn(low, b) + dot_nn(middle, b) + dot_nn(high, b)


def spread(a, beams):
    lane = iota(a.shape, 1)
    base = lane - (lane & (beams - 1))
    return lambda m: jnp.take_along_axis(a, base + m, axis=1, mode="promise_in_bounds")


def complex_product(left_r, left_i, right_r, right_i, beams):
    out_r = out_i = None
    for m in range(beams):
        lr, li = left_r(m), left_i(m)
        rr, ri = right_r[m : m + 1, :], right_i[m : m + 1, :]
        term_r = lr * rr - li * ri
        term_i = lr * ri + li * rr
        out_r = term_r if out_r is None else out_r + term_r
        out_i = term_i if out_i is None else out_i + term_i
    return out_r, out_i


def newton_inverse(gram_r, gram_i, reg_lanes, beams):
    shape = gram_r.shape
    lanes = shape[1]
    shift = log2_of(beams)
    diagonal = (iota(shape, 1) & (beams - 1)) == iota(shape, 0)
    gram_r = gram_r + jnp.where(diagonal, reg_lanes, 0.0)
    diag_row = jnp.sum(jnp.where(diagonal, gram_r, 0.0), axis=0, keepdims=True)
    same = (iota((lanes, lanes), 0) >> shift) == (iota((lanes, lanes), 1) >> shift)
    trace = jnp.dot(
        jnp.broadcast_to(diag_row, (8, lanes)),
        jnp.where(same, 1.0, 0.0),
        precision=HIGH,
        preferred_element_type=F32,
    )[0:1, :]
    first = 1.0 / trace
    start_r = jnp.where(diagonal, 2.0 * first, 0.0) - gram_r * first * first
    start_i = -(gram_i * first * first)
    gather_r, gather_i = spread(gram_r, beams), spread(gram_i, beams)
    held_r = [gather_r(m) for m in range(beams)]
    held_i = [gather_i(m) for m in range(beams)]

    def step(_, carry):
        xr, xi = carry
        yr, yi = complex_product(lambda m: held_r[m], lambda m: held_i[m], xr, xi, beams)
        zr, zi = complex_product(spread(xr, beams), spread(xi, beams), yr, yi, beams)
        return 2.0 * xr - zr, 2.0 * xi - zi

    return lax.fori_loop(1, ITERS, step, (start_r, start_i))


def flip(index, mask, count):
    result = 0
    bit = 1
    while bit < count:
        digit = lax.rem(lax.div(index, bit), 2)
        result = result + bit * (1 - digit if mask & bit else digit)
        bit *= 2
    return result


def kernel(
    dims,
    ch_hbm,
    plan_hbm,
    serving_hbm,
    inter_hbm,
    reg_hbm,
    noise_hbm,
    prec_ref,
    metric_ref,
    rate_ref,
    raw,
    plan_ref,
    inter_ref,
    cells_ref,
    reg_ref,
    noise_ref,
    wide,
    planes,
    columns,
    out_rows,
    in_rows,
    out_more,
    in_more,
    out_ids,
    in_ids,
    own_w,
    all_w,
    forms,
    received,
    pw_own,
    pw_in,
    sc_own,
    sc_in,
    load_sem,
    small_sem,
    row_send,
    row_recv,
    more_send,
    more_recv,
    ids_send,
    ids_recv,
    w_send,
    w_recv,
    pw_send,
    pw_recv,
    sc_send,
    sc_recv,
):
    groups, rb_groups, tracks, blocks, slots, cells, beams, cell_dev, capacity = dims
    entries = cell_dev * blocks * beams
    width = raw.shape[1]
    track_shift = log2_of(tracks)
    beam_shift = log2_of(beams)
    me = lax.axis_index("users")
    my_rb = lax.axis_index("rb")

    rows = raw.shape[0]
    pieces = load_sem.shape[0]
    chunk = rows // pieces
    loads = []
    small = [
        pltpu.make_async_copy(plan_hbm, plan_ref, small_sem.at[0]),
        pltpu.make_async_copy(serving_hbm, cells_ref.at[0], small_sem.at[1]),
        pltpu.make_async_copy(inter_hbm, inter_ref, small_sem.at[2]),
        pltpu.make_async_copy(reg_hbm, reg_ref, small_sem.at[3]),
        pltpu.make_async_copy(noise_hbm, noise_ref, small_sem.at[4]),
    ]
    for copy in small:
        copy.start()
    for i in range(pieces):
        part = pl.ds(i * chunk, chunk)
        copy = pltpu.make_async_copy(ch_hbm.at[part], raw.at[part], load_sem.at[i])
        copy.start()
        loads.append(copy)

    barrier = pltpu.get_barrier_semaphore()
    for offset in range(1, groups):
        pl.semaphore_signal(
            barrier, inc=1, device_id={"users": flip(me, offset, groups)},
            device_id_type=pl.DeviceIdType.MESH,
        )
    for offset in range(1, rb_groups):
        pl.semaphore_signal(
            barrier, inc=1, device_id={"rb": flip(my_rb, offset, rb_groups)},
            device_id_type=pl.DeviceIdType.MESH,
        )

    def user_copy(src, dst, send, recv, offset):
        return pltpu.make_async_remote_copy(
            src_ref=src,
            dst_ref=dst,
            send_sem=send.at[offset],
            recv_sem=recv.at[offset],
            device_id={"users": flip(me, offset, groups)},
            device_id_type=pl.DeviceIdType.MESH,
        )

    for copy in small:
        copy.wait()
    for slot in range(1, slots):
        cells_ref[slot] = inter_ref[slot - 1 : slot, :]
    cell_lanes = blocks * beams
    spread_plan = None
    for block in range(blocks):
        lane = iota((beams, entries), 1) & (cell_lanes - 1)
        put = jnp.where(lane == iota((beams, entries), 0) + block * beams, 1.0, 0.0)
        part = jnp.dot(
            plan_ref[:, block, :].astype(F32), put, precision=HIGH, preferred_element_type=F32
        )
        spread_plan = part if spread_plan is None else spread_plan + part
    ent_f = jnp.zeros((groups, entries), F32)
    for cell in range(cell_dev):
        pick = jnp.where(
            iota((groups, cells), 1) == cell_dev * iota((groups, cells), 0) + cell, 1.0, 0.0
        )
        lane = iota((cells, entries), 1)
        in_cell = (lane >= cell * cell_lanes) & (lane < (cell + 1) * cell_lanes)
        ent_f = ent_f + jnp.dot(
            pick, jnp.where(in_cell, spread_plan, 0.0), precision=HIGH, preferred_element_type=F32
        )
    ent = ent_f.astype(jnp.int32)

    owner = ent >> track_shift
    lane_e = iota((1, entries), 1)
    block_e = (lane_e >> beam_shift) & (blocks - 1)
    code = ((ent & (tracks - 1)) + block_e * tracks + 1).astype(F32)
    before = jnp.where(
        iota((entries, entries), 0) < iota((entries, entries), 1), 1.0, 0.0
    ).astype(BF16)
    mine = jnp.where(owner == me, 1.0, 0.0)
    rank = dot_nn(mine.astype(BF16), before)
    slot_number = iota((capacity, entries), 0).astype(F32)

    def hits_of(flags, ranks, group):
        keep = flags[group : group + 1, :]
        return jnp.where(ranks[group : group + 1, :] == slot_number, keep, 0.0)

    sends = [hits_of(mine, rank, group) for group in range(groups)]
    picks = jnp.concatenate(
        [
            jnp.sum(sends[group] * code[group : group + 1, :], axis=1, keepdims=True)
            for group in range(groups)
        ],
        axis=0,
    ).astype(jnp.int32) - 1

    stride = slots * blocks
    for i in range(pieces):
        loads[i].wait()
        part = slice(i * chunk, (i + 1) * chunk)
        wide[part, :] = raw[part, :].astype(F32)

    def extract(slot):
        for block in range(blocks):
            number = slot * blocks + block
            planes[number] = wide[pl.ds(number, tracks, stride=stride), :].astype(BF16)

    extract(0)

    track_lane = iota((groups * capacity, tracks), 1)
    gathered = None
    hots = []
    for block in range(blocks):
        hots.append(jnp.where(picks - block * tracks == track_lane, 1.0, 0.0).astype(BF16))
        part = dot_nn(hots[block], planes[block])
        gathered = part if gathered is None else gathered + part
    for group in range(groups):
        out_rows[group] = gathered[group * capacity : (group + 1) * capacity].astype(BF16)

    pl.semaphore_wait(barrier, groups - 1 + rb_groups - 1)

    row_copies = []
    for offset in range(1, groups):
        dst = flip(me, offset, groups)
        copy = user_copy(out_rows.at[dst], in_rows.at[me], row_send, row_recv, offset)
        copy.start()
        row_copies.append(copy)
    in_rows[pl.ds(me, 1)] = out_rows[pl.ds(me, 1)]

    for slot in range(1, slots):
        extract(slot)

    gathered = any_hot = None
    for block in range(blocks):
        planes_of = [planes[slot * blocks + block] for slot in range(1, slots)]
        part = dot_nn(hots[block], jnp.concatenate(planes_of, axis=1))
        gathered = part if gathered is None else gathered + part
        any_hot = hots[block] if any_hot is None else any_hot + hots[block]
    heard_rows = [cells_ref[slot].astype(F32) for slot in range(1, slots)]
    heard_rows.append(jnp.zeros((9 - slots, tracks), F32))
    ids = dot_nt(jnp.concatenate(heard_rows, axis=0).astype(BF16), any_hot)
    out_ids[...] = jnp.zeros(out_ids.shape, F32)
    for group in range(groups):
        part = slice(group * capacity, (group + 1) * capacity)
        out_more[group] = gathered[part].astype(BF16)
        out_ids[group, :, 0:capacity] = ids[0 : slots - 1, part]
    more_copies = []
    for offset in range(1, groups):
        dst = flip(me, offset, groups)
        copy = user_copy(out_more.at[dst], in_more.at[me], more_send, more_recv, offset)
        copy.start()
        more_copies.append(copy)
        copy = user_copy(out_ids.at[dst], in_ids.at[me], ids_send, ids_recv, offset)
        copy.start()
        more_copies.append(copy)
    in_more[pl.ds(me, 1)] = out_more[pl.ds(me, 1)]
    in_ids[pl.ds(me, 1)] = out_ids[pl.ds(me, 1)]

    is_me = iota(ent.shape, 0) == me
    my_owner = jnp.sum(jnp.where(is_me, owner.astype(F32), 0.0), axis=0, keepdims=True)
    from_src = jnp.where(my_owner == iota(ent.shape, 0).astype(F32), 1.0, 0.0)
    src_rank = dot_nn(from_src.astype(BF16), before)
    arrivals = [hits_of(from_src, src_rank, group) for group in range(groups)]
    place = jnp.transpose(jnp.concatenate(arrivals, axis=0)).astype(BF16)

    for copy in row_copies:
        copy.wait_recv()
    came = jnp.concatenate([in_rows[group].astype(F32) for group in range(groups)], axis=0)
    sched = dot_nn(place, came.astype(BF16))
    sched_b = sched.astype(BF16)
    turned_b = turn(sched).astype(BF16)

    full_r = dot_nt(sched_b, sched_b)
    full_i = dot_nt(sched_b, turned_b)
    shape = (beams, entries)
    lane_problem = iota(shape, 1) >> beam_shift
    gram_r = gram_i = jnp.zeros(shape, F32)
    for problem in range(cell_dev * blocks):
        part = slice(problem * beams, (problem + 1) * beams)
        here = lane_problem == problem
        gram_r = gram_r + jnp.where(here, full_r[part, :], 0.0)
        gram_i = gram_i + jnp.where(here, full_i[part, :], 0.0)
    reg_lanes = jnp.zeros((1, entries), F32)
    for cell in range(cell_dev):
        reg_lanes = jnp.where(lane_e >= cell * cell_lanes, reg_ref[cell], reg_lanes)
    inv_r, inv_i = newton_inverse(gram_r, gram_i, reg_lanes, beams)

    problems = cell_dev * blocks
    square = (entries, entries)
    same = (iota(square, 0) >> beam_shift) == (iota(square, 1) >> beam_shift)
    wide_r = jnp.where(same, jnp.concatenate([inv_r] * problems, axis=0), 0.0)
    wide_i = jnp.where(same, jnp.concatenate([inv_i] * problems, axis=0), 0.0)
    vectors = dot_split(wide_r, sched_b) + dot_split(wide_i, turned_b)

    cell_shift = log2_of(cell_dev)
    new_row = iota(square, 0)
    old_row = (new_row & (cell_dev - 1)) * cell_lanes + (new_row >> cell_shift)
    order = jnp.where(old_row == iota(square, 1), 1.0, 0.0).astype(BF16)
    unscaled = dot_nn(order, vectors.astype(BF16)).astype(BF16)
    own_w[...] = unscaled
    w_copies = []
    for offset in range(1, groups):
        copy = user_copy(own_w, all_w.at[me], w_send, w_recv, offset)
        copy.start()
        w_copies.append(copy)
    all_w[pl.ds(me, 1)] = unscaled[None]

    squares = vectors * vectors
    sums = [
        jnp.sum(squares[cell * cell_lanes : (cell + 1) * cell_lanes], axis=0, keepdims=True)
        for cell in range(cell_dev)
    ]
    pw_own[...] = jnp.concatenate(sums + [jnp.zeros((8 - cell_dev, width), F32)], axis=0)
    pw_copies = []
    for offset in range(1, rb_groups):
        copy = pltpu.make_async_remote_copy(
            src_ref=pw_own,
            dst_ref=pw_in.at[my_rb],
            send_sem=pw_send.at[offset],
            recv_sem=pw_recv.at[offset],
            device_id={"rb": flip(my_rb, offset, rb_groups)},
            device_id_type=pl.DeviceIdType.MESH,
        )
        copy.start()
        pw_copies.append(copy)
    pw_in[pl.ds(my_rb, 1)] = pw_own[...][None]

    def turn_over(slot, carry):
        for block in range(blocks):
            number = slot * blocks + block
            columns[number] = jnp.transpose(planes[number])
        return carry

    lax.fori_loop(0, slots, turn_over, 0)
    for copy in pw_copies:
        copy.wait_recv()
    total = jnp.sum(jnp.sum(pw_in[...], axis=0), axis=1, keepdims=True)
    scale = lax.rsqrt(total / (blocks * rb_groups) + 1e-06)
    sc_own[...] = jnp.broadcast_to(scale * scale, (8, width))
    sc_copies = []
    for offset in range(1, groups):
        copy = user_copy(sc_own, sc_in.at[me], sc_send, sc_recv, offset)
        copy.start()
        sc_copies.append(copy)
    sc_in[pl.ds(me, 1)] = sc_own[...][None]
    prec = jnp.concatenate(
        [
            vectors[cell * cell_lanes : (cell + 1) * cell_lanes] * scale[cell : cell + 1, :]
            for cell in range(cell_dev)
        ],
        axis=0,
    ).astype(BF16)
    prec_ref[...] = prec

    prec_turned = turn(prec.astype(F32)).astype(BF16)
    z_r = dot_nt(prec, sched_b)
    z_i = dot_nt(prec_turned, sched_b)
    magnitude = jnp.where(same, z_r * z_r + z_i * z_i, 0.0)
    on_diagonal = iota(square, 0) == iota(square, 1)
    signal = jnp.sum(jnp.where(on_diagonal, magnitude, 0.0), axis=0, keepdims=True)
    leakage = jnp.sum(jnp.where(on_diagonal, 0.0, magnitude), axis=0, keepdims=True)

    for copy in more_copies:
        copy.wait_recv()
    came = jnp.concatenate([in_more[group].astype(F32) for group in range(groups)], axis=0)
    more = dot_nn(place, came.astype(BF16))
    entry_rows = jnp.concatenate(
        [more[:, slot * width : (slot + 1) * width] for slot in range(slots - 1)], axis=0
    )
    entry_rows = jnp.transpose(entry_rows).astype(BF16)
    entry_ids = jnp.zeros((slots - 1, entries), F32)
    for group in range(groups):
        known = in_ids[group, :, 0:capacity].astype(BF16)
        entry_ids = entry_ids + dot_nn(known, arrivals[group].astype(BF16))
    entry_heard = jnp.concatenate(
        [entry_ids[slot : slot + 1, :] for slot in range(slots - 1)], axis=1
    ).astype(jnp.int32)
    entry_lanes = (slots - 1) * entries
    entry_block = (iota((1, entry_lanes), 1) >> beam_shift) & (blocks - 1)

    half = groups // 2
    near = lax.div(me, half)
    part_rows = cell_dev * beams
    form_rows = 2 * part_rows

    def heard_power(form, rows, heard):
        lanes = rows.shape[1]
        projected = dot_nn(form, rows)
        energy = jnp.sum(
            (projected * projected).reshape(half, form_rows // 8, 8, lanes), axis=1
        )
        shape = (half, 8, lanes)
        cell = iota(shape, 0) * cell_dev + (iota(shape, 1) & (cell_dev - 1))
        found = jnp.sum(jnp.where(cell == heard[None], energy, 0.0), axis=0)
        return jnp.sum(found, axis=0, keepdims=True)

    entry_power = jnp.zeros((1, entry_lanes), F32)
    for turn_number in range(2):
        for offset in range(1, groups):
            if offset // half == turn_number:
                w_copies[offset - 1].wait_recv()
        first_group = half * (near if turn_number == 0 else 1 - near)
        first_cell = first_group * cell_dev
        for block in range(blocks):
            for group in range(half):
                rows_in = all_w[first_group + group, block * part_rows : (block + 1) * part_rows, :]
                at = group * form_rows
                forms[block, at : at + part_rows, :] = rows_in
                forms[block, at + part_rows : at + form_rows, :] = turn(
                    rows_in.astype(F32)
                ).astype(BF16)

        def track_powers(slot, carry, first_cell=first_cell, keep=turn_number):
            heard = cells_ref[slot] - first_cell
            for block in range(blocks):
                number = slot * blocks + block
                part = heard_power(forms[block], columns[number], heard)
                received[number] = received[number] + part if keep else part
            return carry

        lax.fori_loop(0, slots, track_powers, 0)
        for block in range(blocks):
            part = heard_power(forms[block], entry_rows, entry_heard - first_cell)
            entry_power = entry_power + jnp.where(entry_block == block, part, 0.0)

    for copy in sc_copies:
        copy.wait_recv()

    def scale_row(heard):
        row = jnp.zeros(heard.shape, F32)
        for group in range(groups):
            for cell in range(cell_dev):
                one = sc_in[group, cell : cell + 1, 0:1]
                row = jnp.where(heard == group * cell_dev + cell, one, row)
        return row

    entry_power = entry_power * scale_row(entry_heard)
    entry_denominator = entry_power[:, 0:entries]
    for slot in range(1, slots - 1):
        entry_denominator = entry_denominator + entry_power[:, slot * entries : (slot + 1) * entries]
    noise_lanes = jnp.zeros((1, entries), F32)
    for cell in range(cell_dev):
        noise_lanes = jnp.where(
            lane_e >= cell * cell_lanes, noise_ref[me * cell_dev + cell], noise_lanes
        )
    entry_denominator = entry_denominator + noise_lanes
    rate = jnp.log2(1.0 + signal / (leakage + entry_denominator))
    for cell in range(cell_dev):
        for block in range(blocks):
            start = (cell * blocks + block) * beams
            rate_ref[cell, block : block + 1, :] = rate[:, start : start + beams]

    scales = [scale_row(cells_ref[slot]) for slot in range(slots)]
    floor = jnp.zeros((1, tracks), F32)
    serving = cells_ref[0]
    for cell in range(cells):
        floor = jnp.where(serving == cell, noise_ref[cell], floor)
    for block in range(blocks):
        interference = received[blocks + block] * scales[1]
        for slot in range(2, slots):
            interference = interference + received[slot * blocks + block] * scales[slot]
        power = received[block] * scales[0]
        metric_ref[block : block + 1, :] = jnp.log2(1.0 + power / (interference + floor))

    for copy in row_copies + more_copies + pw_copies + w_copies + sc_copies:
        copy.wait_send()


def hand_over(*refs):
    count = len(refs) // 2
    copies = [
        pltpu.make_async_copy(refs[i], refs[count + i], refs[2 * count].at[i])
        for i in range(count)
    ]
    for copy in copies:
        copy.start()
    for copy in copies:
        copy.wait()


def on_device(channel, serving, interferers, plan, regularizer, noise_floor):
    tracks, blocks, slots, width = channel.shape
    cells, _, beams = plan.shape
    cell_dev = regularizer.shape[0]
    groups = lax.axis_size("users")
    rb_groups = lax.axis_size("rb")
    entries = cell_dev * blocks * beams
    capacity = 2 * entries // groups
    dims = (groups, rb_groups, tracks, blocks, slots, cells, beams, cell_dev, capacity)
    row_count = tracks * slots * blocks
    rows = channel.transpose(0, 2, 1, 3).reshape(row_count, width)
    hbm = pl.BlockSpec(memory_space=pltpu.HBM)
    vmem = pl.BlockSpec(memory_space=pltpu.VMEM)
    dma = pltpu.SemaphoreType.DMA
    results = (
        jax.ShapeDtypeStruct((entries, width), BF16),
        jax.ShapeDtypeStruct((blocks, tracks), F32),
        jax.ShapeDtypeStruct((cell_dev, blocks, beams), F32),
    )
    made = pl.pallas_call(
        functools.partial(kernel, dims),
        out_shape=results,
        in_specs=[hbm] * 6,
        out_specs=(vmem, vmem, vmem),
        scratch_shapes=[
            pltpu.VMEM((row_count, width), BF16),
            pltpu.VMEM((cells, blocks, beams), jnp.int32),
            pltpu.VMEM((slots - 1, tracks), jnp.int32),
            pltpu.VMEM((slots, 1, tracks), jnp.int32),
            pltpu.SMEM(regularizer.shape, F32),
            pltpu.SMEM(noise_floor.shape, F32),
            pltpu.VMEM((row_count, width), F32),
            pltpu.VMEM((slots * blocks, tracks, width), BF16),
            pltpu.VMEM((slots * blocks, width, tracks), BF16),
            pltpu.VMEM((groups, capacity, width), BF16),
            pltpu.VMEM((groups, capacity, width), BF16),
            pltpu.VMEM((groups, capacity, (slots - 1) * width), BF16),
            pltpu.VMEM((groups, capacity, (slots - 1) * width), BF16),
            pltpu.VMEM((groups, slots - 1, width), F32),
            pltpu.VMEM((groups, slots - 1, width), F32),
            pltpu.VMEM((entries, width), BF16),
            pltpu.VMEM((groups, entries, width), BF16),
            pltpu.VMEM((blocks, cells * beams, width), BF16),
            pltpu.VMEM((slots * blocks, 1, tracks), F32),
            pltpu.VMEM((8, width), F32),
            pltpu.VMEM((rb_groups, 8, width), F32),
            pltpu.VMEM((8, width), F32),
            pltpu.VMEM((groups, 8, width), F32),
            dma((8,)),
            dma((5,)),
            *[dma((groups,)) for _ in range(8)],
            dma((rb_groups,)),
            dma((rb_groups,)),
            dma((groups,)),
            dma((groups,)),
        ],
        compiler_params=pltpu.CompilerParams(
            collective_id=0, has_side_effects=True, vmem_limit_bytes=64 << 20
        ),
    )(rows, plan, serving[None, :], interferers.T, regularizer, noise_floor)
    precoders, metric, rate = pl.pallas_call(
        hand_over,
        out_shape=results,
        in_specs=[vmem] * 3,
        out_specs=(hbm, hbm, hbm),
        scratch_shapes=[dma((3,))],
        compiler_params=pltpu.CompilerParams(vmem_limit_bytes=64 << 20),
    )(*made)
    return precoders.reshape(cell_dev, blocks, beams, width), metric.T, rate


def solution(mesh):
    return jax.shard_map(
        on_device,
        mesh=mesh,
        in_specs=(
            P("users", "rb", None, None),
            P("users"),
            P("users", None),
            P(None, "rb", None),
            P("users"),
            P(),
        ),
        out_specs=(P("users", "rb", None, None), P("users", "rb"), P("users", "rb", None)),
        check_vma=False,
    )
```

```python
import functools

import jax
import jax.numpy as jnp
from jax import lax
from jax.experimental import pallas as pl
from jax.experimental.pallas import tpu as pltpu
from jax.sharding import PartitionSpec as P

ITERS = 12
F32 = jnp.float32
BF16 = jnp.bfloat16
HIGH = lax.Precision.HIGHEST


def iota(shape, dim):
    return lax.broadcasted_iota(jnp.int32, shape, dim)


def log2_of(n):
    assert n & (n - 1) == 0
    return n.bit_length() - 1


def turn(rows):
    half = rows.shape[-1] // 2
    sign = jnp.where(iota(rows.shape, 1) < half, 1.0, -1.0)
    return pltpu.roll(rows, half, 1) * sign


def dot_nt(a, b):
    return lax.dot_general(a, b, (((1,), (1,)), ((), ())), preferred_element_type=F32)


def dot_nn(a, b):
    return jnp.dot(a, b, preferred_element_type=F32)


def split3(x):
    high = x.astype(BF16)
    rest = x - high.astype(F32)
    middle = rest.astype(BF16)
    return high, middle, (rest - middle.astype(F32)).astype(BF16)


def dot_split(x, b):
    high, middle, low = split3(x)
    return dot_nn(low, b) + dot_nn(middle, b) + dot_nn(high, b)


def spread(a, beams):
    lane = iota(a.shape, 1)
    base = lane - (lane & (beams - 1))
    return lambda m: jnp.take_along_axis(a, base + m, axis=1, mode="promise_in_bounds")


def complex_product(left_r, left_i, right_r, right_i, beams):
    out_r = out_i = None
    for m in range(beams):
        lr, li = left_r(m), left_i(m)
        rr, ri = right_r[m : m + 1, :], right_i[m : m + 1, :]
        term_r = lr * rr - li * ri
        term_i = lr * ri + li * rr
        out_r = term_r if out_r is None else out_r + term_r
        out_i = term_i if out_i is None else out_i + term_i
    return out_r, out_i


def newton_inverse(gram_r, gram_i, reg_lanes, beams):
    shape = gram_r.shape
    lanes = shape[1]
    shift = log2_of(beams)
    diagonal = (iota(shape, 1) & (beams - 1)) == iota(shape, 0)
    gram_r = gram_r + jnp.where(diagonal, reg_lanes, 0.0)
    diag_row = jnp.sum(jnp.where(diagonal, gram_r, 0.0), axis=0, keepdims=True)
    same = (iota((lanes, lanes), 0) >> shift) == (iota((lanes, lanes), 1) >> shift)
    trace = jnp.dot(
        jnp.broadcast_to(diag_row, (8, lanes)),
        jnp.where(same, 1.0, 0.0),
        precision=HIGH,
        preferred_element_type=F32,
    )[0:1, :]
    first = 1.0 / trace
    start_r = jnp.where(diagonal, 2.0 * first, 0.0) - gram_r * first * first
    start_i = -(gram_i * first * first)
    gather_r, gather_i = spread(gram_r, beams), spread(gram_i, beams)
    held_r = [gather_r(m) for m in range(beams)]
    held_i = [gather_i(m) for m in range(beams)]

    def step(_, carry):
        xr, xi = carry
        yr, yi = complex_product(lambda m: held_r[m], lambda m: held_i[m], xr, xi, beams)
        zr, zi = complex_product(spread(xr, beams), spread(xi, beams), yr, yi, beams)
        return 2.0 * xr - zr, 2.0 * xi - zi

    return lax.fori_loop(1, ITERS, step, (start_r, start_i))


def flip(index, mask, count):
    result = 0
    bit = 1
    while bit < count:
        digit = lax.rem(lax.div(index, bit), 2)
        result = result + bit * (1 - digit if mask & bit else digit)
        bit *= 2
    return result


def kernel(
    dims,
    ch_hbm,
    plan_hbm,
    serving_hbm,
    inter_hbm,
    reg_hbm,
    noise_hbm,
    prec_ref,
    metric_ref,
    rate_ref,
    raw,
    plan_ref,
    inter_ref,
    cells_ref,
    reg_ref,
    noise_ref,
    wide,
    planes,
    out_rows,
    in_rows,
    out_more,
    in_more,
    out_ids,
    in_ids,
    own_w,
    all_w,
    forms,
    received,
    pw_own,
    pw_in,
    sc_own,
    sc_in,
    load_sem,
    small_sem,
    row_send,
    row_recv,
    more_send,
    more_recv,
    ids_send,
    ids_recv,
    w_send,
    w_recv,
    pw_send,
    pw_recv,
    sc_send,
    sc_recv,
):
    groups, rb_groups, tracks, blocks, slots, cells, beams, cell_dev, capacity = dims
    entries = cell_dev * blocks * beams
    width = raw.shape[1]
    track_shift = log2_of(tracks)
    beam_shift = log2_of(beams)
    me = lax.axis_index("users")
    my_rb = lax.axis_index("rb")

    rows = raw.shape[0]
    pieces = load_sem.shape[0]
    chunk = rows // pieces
    loads = []
    small = [
        pltpu.make_async_copy(plan_hbm, plan_ref, small_sem.at[0]),
        pltpu.make_async_copy(serving_hbm, cells_ref.at[0], small_sem.at[1]),
        pltpu.make_async_copy(inter_hbm, inter_ref, small_sem.at[2]),
        pltpu.make_async_copy(reg_hbm, reg_ref, small_sem.at[3]),
        pltpu.make_async_copy(noise_hbm, noise_ref, small_sem.at[4]),
    ]
    for copy in small:
        copy.start()
    for i in range(pieces):
        part = pl.ds(i * chunk, chunk)
        copy = pltpu.make_async_copy(ch_hbm.at[part], raw.at[part], load_sem.at[i])
        copy.start()
        loads.append(copy)

    barrier = pltpu.get_barrier_semaphore()
    for offset in range(1, groups):
        pl.semaphore_signal(
            barrier, inc=1, device_id={"users": flip(me, offset, groups)},
            device_id_type=pl.DeviceIdType.MESH,
        )
    for offset in range(1, rb_groups):
        pl.semaphore_signal(
            barrier, inc=1, device_id={"rb": flip(my_rb, offset, rb_groups)},
            device_id_type=pl.DeviceIdType.MESH,
        )

    def user_copy(src, dst, send, recv, offset):
        return pltpu.make_async_remote_copy(
            src_ref=src,
            dst_ref=dst,
            send_sem=send.at[offset],
            recv_sem=recv.at[offset],
            device_id={"users": flip(me, offset, groups)},
            device_id_type=pl.DeviceIdType.MESH,
        )

    stride = slots * blocks
    for i in range(pieces):
        loads[i].wait()
        part = slice(i * chunk, (i + 1) * chunk)
        wide[part, :] = raw[part, :].astype(F32)

    def extract(slot):
        for block in range(blocks):
            number = slot * blocks + block
            planes[number] = wide[pl.ds(number, tracks, stride=stride), :].astype(BF16)

    extract(0)

    for copy in small:
        copy.wait()
    for slot in range(1, slots):
        cells_ref[slot] = inter_ref[slot - 1 : slot, :]
    cell_lanes = blocks * beams
    spread_plan = None
    for block in range(blocks):
        lane = iota((beams, entries), 1) & (cell_lanes - 1)
        put = jnp.where(lane == iota((beams, entries), 0) + block * beams, 1.0, 0.0).astype(BF16)
        entry = plan_ref[:, block, :]
        halves = jnp.concatenate([entry >> 8, entry & 255], axis=0).astype(F32).astype(BF16)
        part = dot_nn(halves, put)
        spread_plan = part if spread_plan is None else spread_plan + part
    ent_f = jnp.zeros((groups, entries), F32)
    for cell in range(cell_dev):
        pick = jnp.where(
            iota((groups, cells), 1) == cell_dev * iota((groups, cells), 0) + cell, 1.0, 0.0
        ).astype(BF16)
        lane = iota((cells, entries), 1)
        in_cell = (lane >= cell * cell_lanes) & (lane < (cell + 1) * cell_lanes)
        high = jnp.where(in_cell, spread_plan[0:cells], 0.0).astype(BF16)
        low = jnp.where(in_cell, spread_plan[cells : 2 * cells], 0.0).astype(BF16)
        ent_f = ent_f + (256.0 * dot_nn(pick, high) + dot_nn(pick, low))
    ent = ent_f.astype(jnp.int32)

    owner = ent >> track_shift
    lane_e = iota((1, entries), 1)
    block_e = (lane_e >> beam_shift) & (blocks - 1)
    code = ((ent & (tracks - 1)) + block_e * tracks + 1).astype(F32)
    before = jnp.where(
        iota((entries, entries), 0) < iota((entries, entries), 1), 1.0, 0.0
    ).astype(BF16)
    mine = jnp.where(owner == me, 1.0, 0.0)
    rank = dot_nn(mine.astype(BF16), before)
    slot_number = iota((capacity, entries), 0).astype(F32)

    def hits_of(flags, ranks, group):
        keep = flags[group : group + 1, :]
        return jnp.where(ranks[group : group + 1, :] == slot_number, keep, 0.0)

    sends = [hits_of(mine, rank, group) for group in range(groups)]
    picks = jnp.concatenate(
        [
            jnp.sum(sends[group] * code[group : group + 1, :], axis=1, keepdims=True)
            for group in range(groups)
        ],
        axis=0,
    ).astype(jnp.int32) - 1

    track_lane = iota((groups * capacity, tracks), 1)
    gathered = None
    hots = []
    for block in range(blocks):
        hots.append(jnp.where(picks - block * tracks == track_lane, 1.0, 0.0).astype(BF16))
        part = dot_nn(hots[block], planes[block])
        gathered = part if gathered is None else gathered + part
    for group in range(groups):
        out_rows[group] = gathered[group * capacity : (group + 1) * capacity].astype(BF16)

    pl.semaphore_wait(barrier, groups - 1 + rb_groups - 1)

    row_copies = []
    for offset in range(1, groups):
        dst = flip(me, offset, groups)
        copy = user_copy(out_rows.at[dst], in_rows.at[me], row_send, row_recv, offset)
        copy.start()
        row_copies.append(copy)
    in_rows[pl.ds(me, 1)] = out_rows[pl.ds(me, 1)]

    for slot in range(1, slots):
        extract(slot)

    gathered = any_hot = None
    for block in range(blocks):
        planes_of = [planes[slot * blocks + block] for slot in range(1, slots)]
        part = dot_nn(hots[block], jnp.concatenate(planes_of, axis=1))
        gathered = part if gathered is None else gathered + part
        any_hot = hots[block] if any_hot is None else any_hot + hots[block]
    heard_rows = [cells_ref[slot].astype(F32) for slot in range(1, slots)]
    heard_rows.append(jnp.zeros((9 - slots, tracks), F32))
    ids = dot_nt(jnp.concatenate(heard_rows, axis=0).astype(BF16), any_hot)
    out_ids[...] = jnp.zeros(out_ids.shape, F32)
    for group in range(groups):
        part = slice(group * capacity, (group + 1) * capacity)
        out_more[group] = gathered[part].astype(BF16)
        out_ids[group, :, 0:capacity] = ids[0 : slots - 1, part]
    more_copies = []
    for offset in range(1, groups):
        dst = flip(me, offset, groups)
        copy = user_copy(out_more.at[dst], in_more.at[me], more_send, more_recv, offset)
        copy.start()
        more_copies.append(copy)
        copy = user_copy(out_ids.at[dst], in_ids.at[me], ids_send, ids_recv, offset)
        copy.start()
        more_copies.append(copy)
    in_more[pl.ds(me, 1)] = out_more[pl.ds(me, 1)]
    in_ids[pl.ds(me, 1)] = out_ids[pl.ds(me, 1)]

    is_me = iota(ent.shape, 0) == me
    my_owner = jnp.sum(jnp.where(is_me, owner.astype(F32), 0.0), axis=0, keepdims=True)
    from_src = jnp.where(my_owner == iota(ent.shape, 0).astype(F32), 1.0, 0.0)
    src_rank = dot_nn(from_src.astype(BF16), before)
    arrivals = [hits_of(from_src, src_rank, group) for group in range(groups)]
    place = jnp.transpose(jnp.concatenate(arrivals, axis=0)).astype(BF16)

    for copy in row_copies:
        copy.wait_recv()
    came = jnp.concatenate([in_rows[group].astype(F32) for group in range(groups)], axis=0)
    sched = dot_nn(place, came.astype(BF16))
    sched_b = sched.astype(BF16)
    turned_b = turn(sched).astype(BF16)

    full_r = dot_nt(sched_b, sched_b)
    full_i = dot_nt(sched_b, turned_b)
    shape = (beams, entries)
    lane_problem = iota(shape, 1) >> beam_shift
    gram_r = gram_i = jnp.zeros(shape, F32)
    for problem in range(cell_dev * blocks):
        part = slice(problem * beams, (problem + 1) * beams)
        here = lane_problem == problem
        gram_r = gram_r + jnp.where(here, full_r[part, :], 0.0)
        gram_i = gram_i + jnp.where(here, full_i[part, :], 0.0)
    reg_lanes = jnp.zeros((1, entries), F32)
    for cell in range(cell_dev):
        reg_lanes = jnp.where(lane_e >= cell * cell_lanes, reg_ref[cell], reg_lanes)
    inv_r, inv_i = newton_inverse(gram_r, gram_i, reg_lanes, beams)

    problems = cell_dev * blocks
    square = (entries, entries)
    same = (iota(square, 0) >> beam_shift) == (iota(square, 1) >> beam_shift)
    wide_r = jnp.where(same, jnp.concatenate([inv_r] * problems, axis=0), 0.0)
    wide_i = jnp.where(same, jnp.concatenate([inv_i] * problems, axis=0), 0.0)
    vectors = dot_split(wide_r, sched_b) + dot_split(wide_i, turned_b)

    cell_shift = log2_of(cell_dev)
    new_row = iota(square, 0)
    old_row = (new_row & (cell_dev - 1)) * cell_lanes + (new_row >> cell_shift)
    order = jnp.where(old_row == iota(square, 1), 1.0, 0.0).astype(BF16)
    unscaled = dot_nn(order, vectors.astype(BF16)).astype(BF16)
    own_w[...] = unscaled
    w_copies = []
    for offset in range(1, groups):
        copy = user_copy(own_w, all_w.at[me], w_send, w_recv, offset)
        copy.start()
        w_copies.append(copy)
    all_w[pl.ds(me, 1)] = unscaled[None]

    squares = vectors * vectors
    sums = [
        jnp.sum(squares[cell * cell_lanes : (cell + 1) * cell_lanes], axis=0, keepdims=True)
        for cell in range(cell_dev)
    ]
    pw_own[...] = jnp.concatenate(sums + [jnp.zeros((8 - cell_dev, width), F32)], axis=0)
    pw_copies = []
    for offset in range(1, rb_groups):
        copy = pltpu.make_async_remote_copy(
            src_ref=pw_own,
            dst_ref=pw_in.at[my_rb],
            send_sem=pw_send.at[offset],
            recv_sem=pw_recv.at[offset],
            device_id={"rb": flip(my_rb, offset, rb_groups)},
            device_id_type=pl.DeviceIdType.MESH,
        )
        copy.start()
        pw_copies.append(copy)
    pw_in[pl.ds(my_rb, 1)] = pw_own[...][None]
    for copy in pw_copies:
        copy.wait_recv()
    total = jnp.sum(jnp.sum(pw_in[...], axis=0), axis=1, keepdims=True)
    scale = lax.rsqrt(total / (blocks * rb_groups) + 1e-06)
    sc_own[...] = jnp.broadcast_to(scale * scale, (8, width))
    sc_copies = []
    for offset in range(1, groups):
        copy = user_copy(sc_own, sc_in.at[me], sc_send, sc_recv, offset)
        copy.start()
        sc_copies.append(copy)
    sc_in[pl.ds(me, 1)] = sc_own[...][None]
    prec = jnp.concatenate(
        [
            vectors[cell * cell_lanes : (cell + 1) * cell_lanes] * scale[cell : cell + 1, :]
            for cell in range(cell_dev)
        ],
        axis=0,
    ).astype(BF16)
    prec_ref[...] = prec

    prec_turned = turn(prec.astype(F32)).astype(BF16)
    z_r = dot_nt(prec, sched_b)
    z_i = dot_nt(prec_turned, sched_b)
    magnitude = jnp.where(same, z_r * z_r + z_i * z_i, 0.0)
    on_diagonal = iota(square, 0) == iota(square, 1)
    signal = jnp.sum(jnp.where(on_diagonal, magnitude, 0.0), axis=0, keepdims=True)
    leakage = jnp.sum(jnp.where(on_diagonal, 0.0, magnitude), axis=0, keepdims=True)

    for copy in more_copies:
        copy.wait_recv()
    came = jnp.concatenate([in_more[group].astype(F32) for group in range(groups)], axis=0)
    more = dot_nn(place, came.astype(BF16))
    entry_rows = jnp.concatenate(
        [more[:, slot * width : (slot + 1) * width] for slot in range(slots - 1)], axis=0
    ).astype(BF16)
    entry_ids = jnp.zeros((slots - 1, entries), F32)
    for group in range(groups):
        known = in_ids[group, :, 0:capacity].astype(BF16)
        entry_ids = entry_ids + dot_nn(known, arrivals[group].astype(BF16))
    entry_heard = jnp.concatenate(
        [entry_ids[slot : slot + 1, :] for slot in range(slots - 1)], axis=1
    ).astype(jnp.int32)
    entry_lanes = (slots - 1) * entries
    entry_block = (iota((1, entry_lanes), 1) >> beam_shift) & (blocks - 1)

    half = groups // 2
    near = lax.div(me, half)
    part_rows = cell_dev * beams
    form_rows = 2 * part_rows

    def heard_power(form, rows, heard):
        lanes = rows.shape[0]
        projected = dot_nt(form, rows)
        energy = jnp.sum(
            (projected * projected).reshape(half, form_rows // 8, 8, lanes), axis=1
        )
        shape = (half, 8, lanes)
        cell = iota(shape, 0) * cell_dev + (iota(shape, 1) & (cell_dev - 1))
        found = jnp.sum(jnp.where(cell == heard[None], energy, 0.0), axis=0)
        return jnp.sum(found, axis=0, keepdims=True)

    floor = jnp.zeros((1, tracks), F32)
    serving = cells_ref[0]
    for cell in range(cells):
        floor = jnp.where(serving == cell, noise_ref[cell], floor)
    def scale_row(heard):
        row = jnp.zeros(heard.shape, F32)
        for group in range(groups):
            for cell in range(cell_dev):
                one = sc_in[group, cell : cell + 1, 0:1]
                row = jnp.where(heard == group * cell_dev + cell, one, row)
        return row

    entry_power = jnp.zeros((1, entry_lanes), F32)
    for turn_number in range(2):
        if turn_number == 1:
            for copy in sc_copies:
                copy.wait_recv()
            scales = [scale_row(cells_ref[slot]) for slot in range(slots)]
            entry_scale = scale_row(entry_heard)
        for offset in range(1, groups):
            if offset // half == turn_number:
                w_copies[offset - 1].wait_recv()
        first_group = half * (near if turn_number == 0 else 1 - near)
        first_cell = first_group * cell_dev
        for block in range(blocks):
            for group in range(half):
                rows_in = all_w[first_group + group, block * part_rows : (block + 1) * part_rows, :]
                at = group * form_rows
                forms[block, at : at + part_rows, :] = rows_in
                forms[block, at + part_rows : at + form_rows, :] = turn(
                    rows_in.astype(F32)
                ).astype(BF16)

        def track_powers(slot, carry, first_cell=first_cell, keep=turn_number):
            heard = cells_ref[slot] - first_cell
            for block in range(blocks):
                number = slot * blocks + block
                part = heard_power(forms[block], planes[number], heard)
                received[number] = received[number] + part if keep else part
            return carry

        lax.fori_loop(0, slots, track_powers, 0)
        for block in range(blocks):
            part = heard_power(forms[block], entry_rows, entry_heard - first_cell)
            entry_power = entry_power + jnp.where(entry_block == block, part, 0.0)

    entry_power = entry_power * entry_scale
    entry_denominator = entry_power[:, 0:entries]
    for slot in range(1, slots - 1):
        entry_denominator = entry_denominator + entry_power[:, slot * entries : (slot + 1) * entries]
    noise_lanes = jnp.zeros((1, entries), F32)
    for cell in range(cell_dev):
        noise_lanes = jnp.where(
            lane_e >= cell * cell_lanes, noise_ref[me * cell_dev + cell], noise_lanes
        )
    entry_denominator = entry_denominator + noise_lanes
    rate = jnp.log2(1.0 + signal / (leakage + entry_denominator))
    for cell in range(cell_dev):
        for block in range(blocks):
            start = (cell * blocks + block) * beams
            rate_ref[cell, block : block + 1, :] = rate[:, start : start + beams]

    for block in range(blocks):
        interference = received[blocks + block] * scales[1]
        for slot in range(2, slots):
            interference = interference + received[slot * blocks + block] * scales[slot]
        power = received[block] * scales[0]
        metric_ref[block : block + 1, :] = jnp.log2(1.0 + power / (interference + floor))

    for copy in row_copies + more_copies + pw_copies + w_copies + sc_copies:
        copy.wait_send()


def hand_over(*refs):
    count = len(refs) // 2
    copies = [
        pltpu.make_async_copy(refs[i], refs[count + i], refs[2 * count].at[i])
        for i in range(count)
    ]
    for copy in copies:
        copy.start()
    for copy in copies:
        copy.wait()


def on_device(channel, serving, interferers, plan, regularizer, noise_floor):
    tracks, blocks, slots, width = channel.shape
    cells, _, beams = plan.shape
    cell_dev = regularizer.shape[0]
    groups = lax.axis_size("users")
    rb_groups = lax.axis_size("rb")
    entries = cell_dev * blocks * beams
    capacity = 2 * entries // groups
    dims = (groups, rb_groups, tracks, blocks, slots, cells, beams, cell_dev, capacity)
    row_count = tracks * slots * blocks
    rows = channel.transpose(0, 2, 1, 3).reshape(row_count, width)
    hbm = pl.BlockSpec(memory_space=pltpu.HBM)
    vmem = pl.BlockSpec(memory_space=pltpu.VMEM)
    dma = pltpu.SemaphoreType.DMA
    results = (
        jax.ShapeDtypeStruct((entries, width), BF16),
        jax.ShapeDtypeStruct((blocks, tracks), F32),
        jax.ShapeDtypeStruct((cell_dev, blocks, beams), F32),
    )
    made = pl.pallas_call(
        functools.partial(kernel, dims),
        out_shape=results,
        in_specs=[hbm] * 6,
        out_specs=(vmem, vmem, vmem),
        scratch_shapes=[
            pltpu.VMEM((row_count, width), BF16),
            pltpu.VMEM((cells, blocks, beams), jnp.int32),
            pltpu.VMEM((slots - 1, tracks), jnp.int32),
            pltpu.VMEM((slots, 1, tracks), jnp.int32),
            pltpu.SMEM(regularizer.shape, F32),
            pltpu.SMEM(noise_floor.shape, F32),
            pltpu.VMEM((row_count, width), F32),
            pltpu.VMEM((slots * blocks, tracks, width), BF16),
            pltpu.VMEM((groups, capacity, width), BF16),
            pltpu.VMEM((groups, capacity, width), BF16),
            pltpu.VMEM((groups, capacity, (slots - 1) * width), BF16),
            pltpu.VMEM((groups, capacity, (slots - 1) * width), BF16),
            pltpu.VMEM((groups, slots - 1, width), F32),
            pltpu.VMEM((groups, slots - 1, width), F32),
            pltpu.VMEM((entries, width), BF16),
            pltpu.VMEM((groups, entries, width), BF16),
            pltpu.VMEM((blocks, cells * beams, width), BF16),
            pltpu.VMEM((slots * blocks, 1, tracks), F32),
            pltpu.VMEM((8, width), F32),
            pltpu.VMEM((rb_groups, 8, width), F32),
            pltpu.VMEM((8, width), F32),
            pltpu.VMEM((groups, 8, width), F32),
            dma((8,)),
            dma((5,)),
            *[dma((groups,)) for _ in range(8)],
            dma((rb_groups,)),
            dma((rb_groups,)),
            dma((groups,)),
            dma((groups,)),
        ],
        compiler_params=pltpu.CompilerParams(
            collective_id=0, has_side_effects=True, vmem_limit_bytes=64 << 20
        ),
    )(rows, plan, serving[None, :], interferers.T, regularizer, noise_floor)
    precoders, metric, rate = pl.pallas_call(
        hand_over,
        out_shape=results,
        in_specs=[vmem] * 3,
        out_specs=(hbm, hbm, hbm),
        scratch_shapes=[dma((3,))],
        compiler_params=pltpu.CompilerParams(vmem_limit_bytes=64 << 20),
    )(*made)
    return precoders.reshape(cell_dev, blocks, beams, width), metric.T, rate


def solution(mesh):
    return jax.shard_map(
        on_device,
        mesh=mesh,
        in_specs=(
            P("users", "rb", None, None),
            P("users"),
            P("users", None),
            P(None, "rb", None),
            P("users"),
            P(),
        ),
        out_specs=(P("users", "rb", None, None), P("users", "rb"), P("users", "rb", None)),
        check_vma=False,
    )
```
